128 devices in a mesh: row: 8 (over z_lo, y), col: 16 (over z_hi, x, core).
Axes of the slice: x: 4, y: 4, z: 4 (z_hi: 2, z_lo: 2; z = z_hi * 2 + z_lo), core: 2. Of those that a mesh axis runs over, the one named last changes fastest.
Arguments:
- tokens: bfloat16 [512, 256, 512], P('row', 'col'), may hold values from -6 to 6
- cotangent: bfloat16 [512, 256, 512], P('row', 'col'), may hold values from -6 to 6
- gain1: float32 [512], replicated, may hold values from 0.25 to 1.75
- qkv_weight: bfloat16 [1536, 512], replicated, may hold values from -3 to 3, as said below
- proj_weight: bfloat16 [512, 512], replicated, may hold values from -0.25 to 0.25
- gain2: float32 [512], replicated, may hold values from 0.25 to 1.75
- fc1_weight: bfloat16 [2048, 512], replicated, may hold values from -0.25 to 0.25
- fc2_weight: bfloat16 [512, 2048], replicated, may hold values from -0.125 to 0.125
Outputs:
- grad_tokens: bfloat16 [512, 256, 512], P('row', 'col')
- grad_qkv_weight: float32 [1536, 512], P(('row', 'col'))
- grad_proj_weight: float32 [512, 512], P(('row', 'col'))
- grad_fc1_weight: float32 [2048, 512], P(('row', 'col'))
- grad_fc2_weight: float32 [512, 2048], P(('row', 'col'))
- grad_gain1: float32 [512], P(('row', 'col'))
- grad_gain2: float32 [512], P(('row', 'col'))
The draws below stay inside these ranges and needn't reach their ends.
Inputs may be any that keep to these rules, and one draw needn't show every extreme that they name: `qkv_weight`: the query and key rows (rows 0 to 1023) may be up to 2.5 times larger than the value rows.
All inputs are finite; a program needn't handle non-finite values.
Results may differ from the reference program's by a relative error of at most 0.029.
The reference program's roundings to bfloat16 on the way count: a program that leaves them out, or rounds other values in their place, can miss the bound.
Values may be sent and summed in bfloat16 or wider, within the bound.
No kernel may reach another device: no remote copies, remote signals or barrier semaphores. Data moves between devices by JAX's collectives and lax.ppermute only.
A program may use at most 128 MiB of HBM per device.

```python
import jax
import jax.numpy as jnp
from jax import lax

C = 512
HEADS = 16
FF = 2048
WIN = 16
SHIFT = 8
GRID_R = 512
GRID_C = 256


def draw_qkv_weight(key, part):
    key = jax.random.fold_in(key, 11)
    entries = jax.random.normal(key, (3 * C, C), jnp.float32) * C ** (-0.5)
    return entries.astype(jnp.bfloat16)


def levels(rng, extent, pieces, smallest, high):
    level = 1.0
    for dim, shards_of in pieces:
        heights = jax.random.uniform(jax.random.fold_in(jax.random.fold_in(rng, 6), dim), (shards_of,), jnp.float32, smallest / len(pieces), high / len(pieces))
        level = level * jnp.repeat(jnp.exp(heights), extent[dim] // shards_of).reshape((-1,) + (1,) * (len(extent) - 1 - dim))
    return level


def normal_values(rng, extent, width, bound, split=(), held_as=jnp.bfloat16):
    drawn = width * jax.random.normal(rng, extent, jnp.float32)
    if split:
        drawn = drawn * levels(rng, extent, split, -0.22, 0.18)
    return jnp.clip(drawn, -bound, bound).astype(held_as)


def setup_inputs(seed: int = 0) -> dict:
    splits = jax.random.split(jax.random.key(seed), 9)
    tokens = normal_values(splits[0], (GRID_R, GRID_C, C), 1.0, 6.0, ((0, 8), (1, 16)))
    cotangent = normal_values(splits[1], (GRID_R, GRID_C, C), 1.0, 6.0, ((0, 8), (1, 16)))
    gain1 = jnp.clip(1.0 + 0.15 * jax.random.normal(splits[2], (C,), jnp.float32), 0.25, 1.75)
    qkv_weight = draw_qkv_weight(jax.random.fold_in(splits[8], 71), 0)
    proj_weight = normal_values(splits[4], (C, C), C ** -0.5, 0.25)
    gain2 = jnp.clip(1.0 + 0.15 * jax.random.normal(splits[5], (C,), jnp.float32), 0.25, 1.75)
    fc1_weight = normal_values(splits[6], (FF, C), C ** -0.5, 0.25)
    fc2_weight = normal_values(splits[7], (C, FF), FF ** -0.5, 0.125)
    return dict(tokens=tokens, cotangent=cotangent, gain1=gain1, qkv_weight=qkv_weight, proj_weight=proj_weight, gain2=gain2, fc1_weight=fc1_weight, fc2_weight=fc2_weight)


EPS = 1e-05
MASKED = -1000000000.0
ROOT_HALF = 0.7071067811865476
INV_ROOT_TAU = 0.3989422804014327

def normalize(values):
    average = lax.optimization_barrier(jnp.mean(values, axis=-1, keepdims=True))
    centred = values - average
    variance = lax.optimization_barrier(jnp.mean(centred * centred, axis=-1, keepdims=True))
    inverse = lax.rsqrt(variance + EPS)
    return (centred * inverse, inverse)

def norm_back(grad_normed, normed, inverse):
    mean_grad = lax.optimization_barrier(jnp.mean(grad_normed, axis=-1, keepdims=True))
    mean_cross = lax.optimization_barrier(jnp.mean(grad_normed * normed, axis=-1, keepdims=True))
    return (grad_normed - mean_grad - normed * mean_cross) * inverse

def gelu_value(hidden):
    return 0.5 * hidden * (1.0 + lax.erf(hidden * ROOT_HALF))

def gelu_slope(hidden):
    return 0.5 * (1.0 + lax.erf(hidden * ROOT_HALF)) + hidden * INV_ROOT_TAU * jnp.exp(-0.5 * hidden * hidden)

def to_windows(grid):
    grid_rows, grid_cols, channels = grid.shape
    blocks = grid.reshape(grid_rows // WIN, WIN, grid_cols // WIN, WIN, channels)
    return blocks.transpose(0, 2, 1, 3, 4).reshape(-1, WIN * WIN, channels)

def from_windows(windowed, grid_rows, grid_cols):
    channels = windowed.shape[-1]
    blocks = windowed.reshape(grid_rows // WIN, grid_cols // WIN, WIN, WIN, channels)
    return blocks.transpose(0, 2, 1, 3, 4).reshape(grid_rows, grid_cols, channels)

def region(coords, total):
    return jnp.where(coords < total - WIN, 0, jnp.where(coords < total - SHIFT, 1, 2)).astype(jnp.int32)

def split_heads(flat, windows):
    return flat.reshape(windows, WIN * WIN, HEADS, -1)

def window_probs(queries, keys, labels):
    scores = jnp.einsum('qhd,khd->hqk', queries.astype(jnp.float32), keys.astype(jnp.float32))
    allowed = labels[:, None] == labels[None, :]
    scores = jnp.where(allowed[None, :, :], scores, MASKED)
    highest = lax.optimization_barrier(jnp.max(scores, axis=-1, keepdims=True))
    raised = jnp.exp(scores - highest)
    return raised / lax.optimization_barrier(jnp.sum(raised, axis=-1, keepdims=True))

def window_out(window_item):
    queries, keys, values, labels = window_item
    probs_low = window_probs(queries, keys, labels).astype(jnp.bfloat16)
    mixed = jnp.einsum('hqk,khd->qhd', probs_low.astype(jnp.float32), values.astype(jnp.float32))
    return mixed.reshape(mixed.shape[0], -1).astype(jnp.bfloat16)

def window_grad(window_item):
    queries, keys, values, grad_mixed, labels = window_item
    probs = window_probs(queries, keys, labels)
    probs_low = probs.astype(jnp.bfloat16)
    grad_probs = jnp.einsum('qhd,khd->hqk', grad_mixed.astype(jnp.float32), values.astype(jnp.float32))
    grad_values = jnp.einsum('hqk,qhd->khd', probs_low.astype(jnp.float32), grad_mixed.astype(jnp.float32)).astype(jnp.bfloat16)
    grad_scores = probs * (grad_probs - lax.optimization_barrier(jnp.sum(probs * grad_probs, axis=-1, keepdims=True)))
    scores_low = grad_scores.astype(jnp.bfloat16)
    head_scale = queries.shape[-1] ** (-0.5)
    grad_queries = (jnp.einsum('hqk,khd->qhd', scores_low.astype(jnp.float32), keys.astype(jnp.float32)) * head_scale).astype(jnp.bfloat16)
    grad_keys = jnp.einsum('hqk,qhd->khd', scores_low.astype(jnp.float32), queries.astype(jnp.float32)).astype(jnp.bfloat16)
    window_tokens = queries.shape[0]
    return jnp.concatenate([grad_queries.reshape(window_tokens, -1), grad_keys.reshape(window_tokens, -1), grad_values.reshape(window_tokens, -1)], axis=-1)

def block_core(x_tok, dy_tok, labels, gain1, qkv_weight, proj_weight, gain2, fc1_weight, fc2_weight):
    channels = x_tok.shape[-1]
    windows = labels.shape[0]
    head_scale = (channels // HEADS) ** (-0.5)
    normed1, inverse1 = normalize(x_tok.astype(jnp.float32))
    act1 = (normed1 * gain1).astype(jnp.bfloat16)
    projected = jnp.dot(act1, qkv_weight.T, preferred_element_type=jnp.float32)
    queries = (projected[:, :channels] * head_scale).astype(jnp.bfloat16)
    keys = projected[:, channels:2 * channels].astype(jnp.bfloat16)
    values = projected[:, 2 * channels:].astype(jnp.bfloat16)
    head_q = split_heads(queries, windows)
    head_k = split_heads(keys, windows)
    head_v = split_heads(values, windows)
    mixed = lax.map(window_out, (head_q, head_k, head_v, labels)).reshape(-1, channels)
    attn = jnp.dot(mixed, proj_weight.T, preferred_element_type=jnp.float32).astype(jnp.bfloat16)
    resid = x_tok.astype(jnp.float32) + attn.astype(jnp.float32)
    normed2, inverse2 = normalize(resid)
    act2 = (normed2 * gain2).astype(jnp.bfloat16)
    hidden = jnp.dot(act2, fc1_weight.T, preferred_element_type=jnp.float32)
    active = gelu_value(hidden).astype(jnp.bfloat16)
    grad_active = jnp.dot(dy_tok, fc2_weight, preferred_element_type=jnp.float32).astype(jnp.bfloat16)
    grad_hidden = (grad_active.astype(jnp.float32) * gelu_slope(hidden)).astype(jnp.bfloat16)
    grad_act2 = jnp.dot(grad_hidden, fc1_weight, preferred_element_type=jnp.float32)
    grad_resid = dy_tok.astype(jnp.float32) + norm_back(grad_act2 * gain2, normed2, inverse2)
    grad_low = grad_resid.astype(jnp.bfloat16)
    grad_mixed = jnp.dot(grad_low, proj_weight, preferred_element_type=jnp.float32).astype(jnp.bfloat16)
    grad_heads = lax.map(window_grad, (head_q, head_k, head_v, split_heads(grad_mixed, windows), labels)).reshape(-1, 3 * channels)
    grad_act1 = jnp.dot(grad_heads, qkv_weight, preferred_element_type=jnp.float32).astype(jnp.bfloat16)
    dx_tok = (grad_resid + norm_back(grad_act1.astype(jnp.float32) * gain1, normed1, inverse1)).astype(jnp.bfloat16)
    terms = (jnp.dot(grad_heads.T, act1, preferred_element_type=jnp.float32), jnp.dot(grad_low.T, mixed, preferred_element_type=jnp.float32), jnp.dot(grad_hidden.T, act2, preferred_element_type=jnp.float32), jnp.dot(dy_tok.T, active, preferred_element_type=jnp.float32), lax.optimization_barrier(jnp.sum(grad_act1.astype(jnp.float32) * normed1, axis=0)), lax.optimization_barrier(jnp.sum(grad_act2 * normed2, axis=0)))
    return (dx_tok, terms)

def reference(tokens, cotangent, gain1, qkv_weight, proj_weight, gain2, fc1_weight, fc2_weight):
    total_rows, total_cols, channels = tokens.shape
    rolled_x = jnp.roll(tokens, (-SHIFT, -SHIFT), axis=(0, 1))
    rolled_g = jnp.roll(cotangent, (-SHIFT, -SHIFT), axis=(0, 1))
    strips = total_rows // WIN
    x_strips = rolled_x.reshape(strips, WIN, total_cols, channels)
    g_strips = rolled_g.reshape(strips, WIN, total_cols, channels)
    col_labels = region(jnp.arange(total_cols, dtype=jnp.int32), total_cols)

    def strip_step(totals, strip_item):
        x_strip, g_strip, strip_index = strip_item
        row_labels = region(strip_index * WIN + jnp.arange(WIN, dtype=jnp.int32), total_rows)
        label_grid = 3 * row_labels[:, None] + col_labels[None, :]
        labels = to_windows(label_grid[:, :, None])[:, :, 0]
        windows = labels.shape[0]
        dx_tok, terms = block_core(to_windows(x_strip).reshape(-1, channels), to_windows(g_strip).reshape(-1, channels), labels, gain1, qkv_weight, proj_weight, gain2, fc1_weight, fc2_weight)
        totals = tuple((held + term for held, term in zip(totals, terms)))
        return (totals, from_windows(dx_tok.reshape(windows, -1, channels), WIN, total_cols))
    start_sums = (jnp.zeros(qkv_weight.shape, jnp.float32), jnp.zeros(proj_weight.shape, jnp.float32), jnp.zeros(fc1_weight.shape, jnp.float32), jnp.zeros(fc2_weight.shape, jnp.float32), jnp.zeros((channels,), jnp.float32), jnp.zeros((channels,), jnp.float32))
    sums, dx_strips = lax.scan(strip_step, start_sums, (x_strips, g_strips, jnp.arange(strips, dtype=jnp.int32)))
    grad_tokens = jnp.roll(dx_strips.reshape(total_rows, total_cols, channels), (SHIFT, SHIFT), axis=(0, 1))
    norm_factor = (total_rows * total_cols) ** (-0.5)
    return (grad_tokens, sums[0] * norm_factor, sums[1] * norm_factor, sums[2] * norm_factor, sums[3] * norm_factor, sums[4] * norm_factor, sums[5] * norm_factor)
```

```python
import functools

import jax
import jax.numpy as jnp
from jax import lax
from jax.experimental import pallas as pl
from jax.experimental.pallas import tpu as pltpu
from jax.sharding import Mesh, PartitionSpec as P

HEADS = 16
WIN = 16
SHIFT = 8

EPS = 1e-05
MASKED = -1000000000.0
ROOT_HALF = 0.7071067811865476
INV_ROOT_TAU = 0.3989422804014327

F32 = jnp.float32
BF16 = jnp.bfloat16
ROWS = ("zl", "y")
COLS = ("zh", "x", "core")
CHIPS = ("zl", "y", "zh", "x")
ALL = ROWS + COLS


def nn(a, b):
    return lax.dot_general(a, b, (((1,), (0,)), ((), ())), preferred_element_type=F32)


def nt(a, b):
    return lax.dot_general(a, b, (((1,), (1,)), ((), ())), preferred_element_type=F32)


def tn(a, b):
    return lax.dot_general(a, b, (((0,), (0,)), ((), ())), preferred_element_type=F32)


def ring(block, axes, distance):
    size = 1
    for axis in axes:
        size *= lax.axis_size(axis)
    route = [((i - distance) % size, i) for i in range(size)]
    return lax.ppermute(block, axes, route)


def norm_stats(values):
    average = jnp.mean(values, axis=0, keepdims=True)
    centred = values - average
    variance = jnp.mean(centred * centred, axis=0, keepdims=True)
    inverse = lax.rsqrt(variance + EPS)
    return centred * inverse, inverse


def norm_back(grad_normed, normed, inverse):
    mean_grad = jnp.mean(grad_normed, axis=0, keepdims=True)
    mean_cross = jnp.mean(grad_normed * normed, axis=0, keepdims=True)
    return (grad_normed - mean_grad - normed * mean_cross) * inverse


def forward_kernel(
    x_ref, qkv_ref, proj_ref, gain1_ref, gain2_ref, lab_row_ref, lab_col_ref,
    heads_ref, mixed_ref, act1_ref, normed1_ref, inv1_ref, lse_ref, normed2_ref, inv2_ref, act2_ref,
    mask_ref,
):
    channels = x_ref.shape[1]
    head_dim = channels // HEADS
    x = x_ref[...].astype(F32).T
    normed1, inverse1 = norm_stats(x)
    act1 = (normed1 * gain1_ref[...]).astype(BF16)
    act1_ref[...] = act1
    normed1_ref[...] = normed1
    inv1_ref[...] = inverse1
    queries = nn(qkv_ref[pl.ds(0, channels), :], act1) * (head_dim ** (-0.5))
    heads_ref[pl.ds(0, channels), :] = queries.astype(BF16)
    heads_ref[pl.ds(channels, 2 * channels), :] = nn(
        qkv_ref[pl.ds(channels, 2 * channels), :], act1
    ).astype(BF16)
    mask_ref[...] = (lab_col_ref[0] == lab_row_ref[0]).astype(F32)
    for head in range(HEADS):
        at = head * head_dim
        query = heads_ref[pl.ds(at, head_dim), :]
        key = heads_ref[pl.ds(channels + at, head_dim), :]
        value = heads_ref[pl.ds(2 * channels + at, head_dim), :]
        scores = jnp.where(mask_ref[...] > 0.5, tn(key, query), MASKED)
        highest = jnp.max(scores, axis=0, keepdims=True)
        raised = jnp.exp(scores - highest)
        total = jnp.sum(raised, axis=0, keepdims=True)
        probs_low = (raised * (1.0 / total)).astype(BF16)
        lse_ref[0, pl.ds(head, 1), :] = highest + jnp.log(total)
        mixed_ref[pl.ds(at, head_dim), :] = nn(value, probs_low).astype(BF16)
    attn = nn(proj_ref[...], mixed_ref[...]).astype(BF16)
    normed2, inverse2 = norm_stats(x + attn.astype(F32))
    normed2_ref[...] = normed2
    inv2_ref[...] = inverse2
    act2_ref[...] = (normed2 * gain2_ref[...]).astype(BF16)


def forward(x_win, qkv_weight, proj_weight, gain1, gain2, labels):
    tokens, channels = x_win.shape
    window = WIN * WIN
    windows = tokens // window
    whole = lambda shape: pl.BlockSpec(shape, lambda w: (0,) * len(shape))
    feature = lambda rows: pl.BlockSpec((rows, window), lambda w: (0, w))
    return pl.pallas_call(
        forward_kernel,
        grid=(windows,),
        in_specs=[
            pl.BlockSpec((window, channels), lambda w: (w, 0)),
            whole(qkv_weight.shape),
            whole(proj_weight.shape),
            whole((channels, 1)),
            whole((channels, 1)),
            pl.BlockSpec((1, 1, window), lambda w: (w, 0, 0)),
            pl.BlockSpec((1, window, 1), lambda w: (w, 0, 0)),
        ],
        out_specs=[
            feature(3 * channels),
            feature(channels),
            feature(channels),
            feature(channels),
            feature(1),
            pl.BlockSpec((1, HEADS, window), lambda w: (w, 0, 0)),
            feature(channels),
            feature(1),
            feature(channels),
        ],
        out_shape=[
            jax.ShapeDtypeStruct((3 * channels, tokens), BF16),
            jax.ShapeDtypeStruct((channels, tokens), BF16),
            jax.ShapeDtypeStruct((channels, tokens), BF16),
            jax.ShapeDtypeStruct((channels, tokens), F32),
            jax.ShapeDtypeStruct((1, tokens), F32),
            jax.ShapeDtypeStruct((windows, HEADS, window), F32),
            jax.ShapeDtypeStruct((channels, tokens), F32),
            jax.ShapeDtypeStruct((1, tokens), F32),
            jax.ShapeDtypeStruct((channels, tokens), BF16),
        ],
        scratch_shapes=[pltpu.VMEM((window, window), F32)],
        compiler_params=pltpu.CompilerParams(vmem_limit_bytes=60 * 2**20),
        name="attention_forward",
    )(
        x_win, qkv_weight, proj_weight, gain1[:, None], gain2[:, None],
        labels[:, None, :], labels[:, :, None],
    )


def feed_forward_kernel(
    core_ref, g_ref, act2_ref, normed2_ref, inv2_ref, gain2_ref, fc1_ref, fc2_ref,
    parts_ref, resid_ref, low_ref, gain_ref,
    g_t_ref, sum_ref, fc2_sum_ref,
):
    step = pl.program_id(0)
    core = core_ref[0]
    channels, tokens = act2_ref.shape
    chunk = fc1_ref.shape[0]
    rows = 32

    @pl.when(step == 0)
    def _():
        g_t_ref[...] = g_ref[...].astype(F32).T.astype(BF16)
        sum_ref[...] = jnp.zeros_like(sum_ref)

    piece = 256
    actives = []
    hiddens = []
    for at in range(0, tokens, piece):
        span = pl.ds(at, piece)
        hidden = nn(fc1_ref[...], act2_ref[:, span])
        grad_active = tn(fc2_ref[...], g_t_ref[:, span]).astype(BF16).astype(F32)
        bell = 0.5 * (1.0 + lax.erf(hidden * ROOT_HALF))
        actives.append((hidden * bell).astype(BF16))
        slope = bell + hidden * INV_ROOT_TAU * jnp.exp(-0.5 * hidden * hidden)
        grad_hidden = (grad_active * slope).astype(BF16)
        hiddens.append(grad_hidden)
        sum_ref[:, span] += tn(fc1_ref[...], grad_hidden)
    active = jnp.concatenate(actives, axis=1)
    grad_hidden = jnp.concatenate(hiddens, axis=1)
    fc1_part = nt(grad_hidden, act2_ref[...]).astype(BF16)
    fc2_sum_ref[step] = nt(g_t_ref[...], active)
    for group in range(chunk // 16):
        at = step * (chunk // 32 * rows) + (group // 2) * rows
        parts_ref[core ^ (group % 2), pl.ds(pl.multiple_of(at, rows), 16), :] = fc1_part[
            group * 16 : (group + 1) * 16
        ]

    @pl.when(step == pl.num_programs(0) - 1)
    def _():
        grad_act2 = sum_ref[...]
        normed2 = normed2_ref[...]
        gain_ref[...] = jnp.sum(grad_act2 * normed2, axis=1, keepdims=True)
        grad_resid = g_t_ref[...].astype(F32) + norm_back(
            grad_act2 * gain2_ref[...], normed2, inv2_ref[...]
        )
        resid_ref[...] = grad_resid
        low_ref[...] = grad_resid.astype(BF16)

        @pl.loop(0, channels // 8)
        def _(pair):
            at = pl.ds(pl.multiple_of(pair * 8, 8), 8)
            taken = [fc2_sum_ref[s, at, :] for s in range(4)]
            to = pl.ds(pl.multiple_of(pair * rows + 16, 16), 16)
            for place in range(2):
                block = jnp.concatenate([t[4 * place : 4 * place + 4] for t in taken], axis=0)
                parts_ref[core ^ place, to, :] = block.astype(BF16)


def feed_forward(core, g_win, act2, normed2, inv2, gain2, fc1_weight, fc2_weight):
    tokens, channels = g_win.shape
    hidden = fc1_weight.shape[0]
    chunk = 512
    whole = lambda shape: pl.BlockSpec(shape, lambda s: (0,) * len(shape))
    return pl.pallas_call(
        feed_forward_kernel,
        grid=(hidden // chunk,),
        in_specs=[
            pl.BlockSpec(memory_space=pltpu.SMEM),
            whole((tokens, channels)),
            whole((channels, tokens)),
            whole((channels, tokens)),
            whole((1, tokens)),
            whole((channels, 1)),
            pl.BlockSpec((chunk, channels), lambda s: (s, 0)),
            pl.BlockSpec((channels, chunk), lambda s: (0, s)),
        ],
        out_specs=[
            whole((2, hidden, channels)),
            whole((channels, tokens)),
            whole((channels, tokens)),
            whole((channels, 1)),
        ],
        out_shape=[
            jax.ShapeDtypeStruct((2, hidden, channels), BF16),
            jax.ShapeDtypeStruct((channels, tokens), F32),
            jax.ShapeDtypeStruct((channels, tokens), BF16),
            jax.ShapeDtypeStruct((channels, 1), F32),
        ],
        scratch_shapes=[
            pltpu.VMEM((channels, tokens), BF16),
            pltpu.VMEM((channels, tokens), F32),
            pltpu.VMEM((hidden // chunk, channels, chunk), F32),
        ],
        compiler_params=pltpu.CompilerParams(vmem_limit_bytes=60 * 2**20),
        name="feed_forward",
    )(core, g_win, act2, normed2, inv2, gain2[:, None], fc1_weight, fc2_weight)


def backward_kernel(
    core_ref, low_ref, resid_ref, heads_ref, mixed_ref, lse_ref, act1_ref, normed1_ref, inv1_ref,
    gain1_ref, gain2_sum_ref, qkv_ref, proj_ref, lab_row_ref, lab_col_ref,
    dx_ref, parts_ref,
    mask_ref, grad_mixed_ref, grad_heads_ref, qkv_sum_ref, proj_sum_ref, gain_ref, qkv_t_ref, proj_t_ref,
    gains_ref,
):
    step = pl.program_id(0)
    core = core_ref[0]
    channels = low_ref.shape[0]
    head_dim = channels // HEADS

    @pl.when(step == 0)
    def _():
        qkv_sum_ref[...] = jnp.zeros_like(qkv_sum_ref)
        proj_sum_ref[...] = jnp.zeros_like(proj_sum_ref)
        gain_ref[...] = jnp.zeros_like(gain_ref)
        qkv_t_ref[...] = qkv_ref[...].T
        proj_t_ref[...] = proj_ref[...].T

    grad_mixed_ref[...] = nn(proj_t_ref[...], low_ref[...]).astype(BF16)
    proj_sum_ref[...] += nt(low_ref[...], mixed_ref[...])
    mask_ref[...] = (lab_col_ref[0] == lab_row_ref[0]).astype(F32)
    for head in range(HEADS):
        at = head * head_dim
        query = heads_ref[pl.ds(at, head_dim), :]
        key = heads_ref[pl.ds(channels + at, head_dim), :]
        value = heads_ref[pl.ds(2 * channels + at, head_dim), :]
        grad_mixed = grad_mixed_ref[pl.ds(at, head_dim), :]
        scores = jnp.where(mask_ref[...] > 0.5, tn(key, query), MASKED)
        probs = jnp.exp(scores - lse_ref[0, pl.ds(head, 1), :])
        grad_probs = tn(value, grad_mixed)
        cross = jnp.sum(probs * grad_probs, axis=0, keepdims=True)
        scores_low = (probs * (grad_probs - cross)).astype(BF16)
        grad_heads_ref[pl.ds(2 * channels + at, head_dim), :] = nt(
            grad_mixed, probs.astype(BF16)
        ).astype(BF16)
        grad_heads_ref[pl.ds(at, head_dim), :] = (
            nn(key, scores_low) * (head_dim ** (-0.5))
        ).astype(BF16)
        grad_heads_ref[pl.ds(channels + at, head_dim), :] = nt(query, scores_low).astype(BF16)
    grad_heads = grad_heads_ref[...]
    qkv_sum_ref[...] += nt(grad_heads, act1_ref[...])
    grad_act1 = nn(qkv_t_ref[...], grad_heads).astype(BF16).astype(F32)
    normed1 = normed1_ref[...]
    gain_ref[...] += jnp.sum(grad_act1 * normed1, axis=1, keepdims=True)
    dx = resid_ref[...] + norm_back(grad_act1 * gain1_ref[...], normed1, inv1_ref[...])
    dx_ref[...] = dx.T.astype(BF16)

    @pl.when(step == pl.num_programs(0) - 1)
    def _():
        lanes = lax.broadcasted_iota(jnp.int32, (channels, 128), 1)
        gains = jnp.where(
            lanes == 0, gain_ref[...], jnp.where(lanes == 1, gain2_sum_ref[...], 0.0)
        )
        gains_ref[...] = gains

        @pl.loop(0, channels // 8)
        def _(pair):
            at = pl.ds(pl.multiple_of(pair * 8, 8), 8)
            qkv = qkv_sum_ref[pl.ds(pl.multiple_of(pair * 24, 8), 24), :]
            proj = proj_sum_ref[at, :]
            gain = gains_ref[at, :]
            to = pl.ds(pl.multiple_of(pair * 16, 16), 16)
            for place in range(2):
                four = slice(4 * place, 4 * place + 4)
                block = jnp.concatenate([qkv[12 * place : 12 * place + 12], proj[four]], axis=0)
                parts_ref[core ^ place, to, pl.ds(0, channels)] = block.astype(BF16)
                side = jnp.concatenate([jnp.zeros((12, 128), F32), gain[four]], axis=0)
                parts_ref[core ^ place, to, pl.ds(channels, 128)] = side.astype(BF16)


def backward(
    core, low, resid, heads, mixed, lse, act1, normed1, inv1, gain1, gain2_sum, qkv_weight, proj_weight,
    labels,
):
    channels, tokens = low.shape
    window = WIN * WIN
    windows = tokens // window
    whole = lambda shape: pl.BlockSpec(shape, lambda w: (0,) * len(shape))
    feature = lambda rows: pl.BlockSpec((rows, window), lambda w: (0, w))
    return pl.pallas_call(
        backward_kernel,
        grid=(windows,),
        in_specs=[
            pl.BlockSpec(memory_space=pltpu.SMEM),
            feature(channels),
            feature(channels),
            feature(3 * channels),
            feature(channels),
            pl.BlockSpec((1, HEADS, window), lambda w: (w, 0, 0)),
            feature(channels),
            feature(channels),
            feature(1),
            whole((channels, 1)),
            whole((channels, 1)),
            whole(qkv_weight.shape),
            whole(proj_weight.shape),
            pl.BlockSpec((1, 1, window), lambda w: (w, 0, 0)),
            pl.BlockSpec((1, window, 1), lambda w: (w, 0, 0)),
        ],
        out_specs=[
            pl.BlockSpec((window, channels), lambda w: (w, 0)),
            whole((2, 2 * channels, channels + 128)),
        ],
        out_shape=[
            jax.ShapeDtypeStruct((tokens, channels), BF16),
            jax.ShapeDtypeStruct((2, 2 * channels, channels + 128), BF16),
        ],
        scratch_shapes=[
            pltpu.VMEM((window, window), F32),
            pltpu.VMEM((channels, window), BF16),
            pltpu.VMEM((3 * channels, window), BF16),
            pltpu.VMEM((3 * channels, channels), F32),
            pltpu.VMEM((channels, channels), F32),
            pltpu.VMEM((channels, 1), F32),
            pltpu.VMEM((channels, 3 * channels), BF16),
            pltpu.VMEM((channels, channels), BF16),
            pltpu.VMEM((channels, 128), F32),
        ],
        compiler_params=pltpu.CompilerParams(vmem_limit_bytes=60 * 2**20),
        name="attention_backward",
    )(
        core, low, resid, heads, mixed, lse, act1, normed1, inv1, gain1[:, None], gain2_sum,
        qkv_weight, proj_weight, labels[:, None, :], labels[:, :, None],
    )


def region(coords, total):
    return jnp.where(coords < total - WIN, 0, jnp.where(coords < total - SHIFT, 1, 2)).astype(
        jnp.int32
    )


def to_windows(grid):
    grid_rows, grid_cols = grid.shape
    blocks = grid.reshape(grid_rows // WIN, WIN, grid_cols // WIN, WIN)
    return blocks.transpose(0, 2, 1, 3).reshape(-1, WIN * WIN)


def diagonal(block):
    rows = lax.axis_size("zl") * lax.axis_size("y")
    cols = lax.axis_size("zh") * lax.axis_size("x") * lax.axis_size("core")
    route = [
        ((r + 1) % rows * cols + (c + 1) % cols, r * cols + c) for r in range(rows) for c in range(cols)
    ]
    return lax.ppermute(block, ALL, route)


def roll_in(grid):
    beside = ring(grid[:, :SHIFT], COLS, -1)
    below = ring(grid[:SHIFT, SHIFT:], ROWS, -1)
    corner = diagonal(grid[:SHIFT, :SHIFT])
    left = jnp.concatenate([grid[SHIFT:, SHIFT:], below], axis=0)
    right = jnp.concatenate([beside[SHIFT:], corner], axis=0)
    return jnp.concatenate([left, right], axis=1)


def roll_out(grid):
    above = ring(grid[-SHIFT:], ROWS, 1)
    rows_done = jnp.concatenate([above, grid[:-SHIFT]], axis=0)
    before = ring(rows_done[:, -SHIFT:], COLS, 1)
    return jnp.concatenate([before, rows_done[:, :-SHIFT]], axis=1)


def core_sum(parts):
    got = lax.ppermute(parts[1], "core", [(0, 1), (1, 0)])
    return (parts[0].astype(F32) + got.astype(F32)).astype(BF16)


def chips_sum(part):
    chips = 1
    for axis in CHIPS:
        chips *= lax.axis_size(axis)
    blocks = part.reshape(chips, -1, part.shape[1])
    return lax.all_to_all(blocks, CHIPS, 0, 0, tiled=True).astype(F32).sum(0)


def shards(tokens, cotangent, gain1, qkv_weight, proj_weight, gain2, fc1_weight, fc2_weight):
    tile_rows, tile_cols, channels = tokens.shape
    devices = 1
    for axis in ALL:
        devices *= lax.axis_size(axis)
    rows_total = tile_rows * lax.axis_size("zl") * lax.axis_size("y")
    cols_total = tile_cols * (devices * tile_rows // rows_total)
    row_at = lax.axis_index(ROWS) * tile_rows
    col_at = lax.axis_index(COLS) * tile_cols
    row_coords = row_at + jnp.arange(tile_rows, dtype=jnp.int32)
    col_coords = col_at + jnp.arange(tile_cols, dtype=jnp.int32)
    labels = to_windows(
        3 * region(row_coords, rows_total)[:, None] + region(col_coords, cols_total)[None, :]
    )
    x_win = roll_in(tokens).reshape(-1, channels)
    g_win = roll_in(cotangent).reshape(-1, channels)
    heads, mixed, act1, normed1, inv1, lse, normed2, inv2, act2 = forward(
        x_win, qkv_weight, proj_weight, gain1, gain2, labels
    )
    core = lax.axis_index("core").astype(jnp.int32).reshape(1)
    ffn_parts, resid, low, gain2_sum = feed_forward(
        core, g_win, act2, normed2, inv2, gain2, fc1_weight, fc2_weight
    )
    ffn_chip = core_sum(ffn_parts)
    low, ffn_chip = lax.optimization_barrier((low, ffn_chip))
    ffn = chips_sum(ffn_chip)
    dx, att_parts = backward(
        core, low, resid, heads, mixed, lse, act1, normed1, inv1, gain1, gain2_sum, qkv_weight,
        proj_weight, labels,
    )
    att = chips_sum(core_sum(att_parts))
    grad_tokens = roll_out(dx.reshape(tile_rows, tile_cols, channels))
    norm_factor = (rows_total * cols_total) ** (-0.5)
    ffn = ffn * norm_factor
    att = att * norm_factor
    fc1_rows = fc1_weight.shape[0] // devices
    qkv_rows = qkv_weight.shape[0] // devices
    return (
        grad_tokens,
        att[:qkv_rows, :channels],
        att[qkv_rows:, :channels],
        ffn[:fc1_rows],
        ffn[fc1_rows:].reshape(4, 4, channels).transpose(1, 0, 2).reshape(4, -1),
        att[qkv_rows:, channels],
        att[qkv_rows:, channels + 1],
    )


def solution(mesh):
    fine = Mesh(mesh.devices.reshape(2, 4, 2, 4, 2), ALL)
    return jax.shard_map(
        shards,
        mesh=fine,
        in_specs=(P(ROWS, COLS, None), P(ROWS, COLS, None), P(), P(), P(), P(), P(), P()),
        out_specs=(
            P(ROWS, COLS, None),
            P(ALL, None),
            P(ALL, None),
            P(ALL, None),
            P(ALL, None),
            P(ALL),
            P(ALL),
        ),
        check_vma=False,
    )
```

```python
import functools

import jax
import jax.numpy as jnp
from jax import lax
from jax.experimental import pallas as pl
from jax.experimental.pallas import tpu as pltpu
from jax.sharding import Mesh, PartitionSpec as P

HEADS = 16
WIN = 16
SHIFT = 8

EPS = 1e-05
MASKED = -1000000000.0
ROOT_HALF = 0.7071067811865476
INV_ROOT_TAU = 0.3989422804014327

F32 = jnp.float32
BF16 = jnp.bfloat16
ROWS = ("zl", "y")
COLS = ("zh", "x", "core")
CHIPS = ("zl", "y", "zh", "x")
ALL = ROWS + COLS


def nn(a, b):
    return lax.dot_general(a, b, (((1,), (0,)), ((), ())), preferred_element_type=F32)


def nt(a, b):
    return lax.dot_general(a, b, (((1,), (1,)), ((), ())), preferred_element_type=F32)


def tn(a, b):
    return lax.dot_general(a, b, (((0,), (0,)), ((), ())), preferred_element_type=F32)


def ring(block, axes, distance):
    size = 1
    for axis in axes:
        size *= lax.axis_size(axis)
    route = [((i - distance) % size, i) for i in range(size)]
    return lax.ppermute(block, axes, route)


def norm_stats(values):
    average = jnp.mean(values, axis=0, keepdims=True)
    centred = values - average
    variance = jnp.mean(centred * centred, axis=0, keepdims=True)
    inverse = lax.rsqrt(variance + EPS)
    return centred * inverse, inverse


def norm_back(grad_normed, normed, inverse):
    mean_grad = jnp.mean(grad_normed, axis=0, keepdims=True)
    mean_cross = jnp.mean(grad_normed * normed, axis=0, keepdims=True)
    return (grad_normed - mean_grad - normed * mean_cross) * inverse


def staged(count, lead, first, second, third):
    opened, closed = {}, {}
    for turn in range(count + lead + 1):
        if turn < count:
            opened[turn] = first(turn)
        if 0 <= turn - lead < count:
            closed[turn - lead] = second(turn - lead, opened.pop(turn - lead))
        if 0 <= turn - lead - 1 < count:
            third(turn - lead - 1, closed.pop(turn - lead - 1))


def by_place(core, emit):
    for place in range(2):

        @pl.when(core == place)
        def _():
            emit(place)


def region(coords, total):
    return jnp.where(coords < total - WIN, 0, jnp.where(coords < total - SHIFT, 1, 2)).astype(
        jnp.int32
    )


def column(row, copies):
    block = jnp.broadcast_to(row, (128, row.shape[1])).T
    return jnp.concatenate([block] * copies, axis=1)


def same_region(place_ref, window, totals):
    def labels(shape, dim):
        token = lax.broadcasted_iota(jnp.int32, shape, dim)
        down = place_ref[1] + window * WIN + token // WIN
        along = place_ref[2] + token % WIN
        return 3 * region(down, totals[0]) + region(along, totals[1])

    tokens = WIN * WIN
    return (labels((tokens, tokens), 0) == labels((tokens, tokens), 1)).astype(F32)


def forward_kernel(
    totals, place_ref, x_ref, qkv_ref, proj_ref, gain1_ref, gain2_ref,
    heads_ref, mixed_ref, act1_ref, normed1_ref, inv1_ref, lse_ref, normed2_ref, inv2_ref, act2_ref,
    mask_ref,
):
    channels = x_ref.shape[1]
    head_dim = channels // HEADS
    x = x_ref[...].astype(F32).T
    normed1, inverse1 = norm_stats(x)
    act1 = (normed1 * column(gain1_ref[...], 2)).astype(BF16)
    act1_ref[...] = act1
    normed1_ref[...] = normed1
    inv1_ref[...] = inverse1
    queries = nn(qkv_ref[pl.ds(0, channels), :], act1) * (head_dim ** (-0.5))
    heads_ref[pl.ds(0, channels), :] = queries.astype(BF16)
    heads_ref[pl.ds(channels, 2 * channels), :] = nn(
        qkv_ref[pl.ds(channels, 2 * channels), :], act1
    ).astype(BF16)
    mask_ref[...] = same_region(place_ref, pl.program_id(0), totals)

    def score(head):
        at = head * head_dim
        return tn(heads_ref[pl.ds(channels + at, head_dim), :], heads_ref[pl.ds(at, head_dim), :])

    def soften(head, scores):
        scores = jnp.where(mask_ref[...] > 0.5, scores, MASKED)
        highest = jnp.max(scores, axis=0, keepdims=True)
        raised = jnp.exp(scores - highest)
        total = jnp.sum(raised, axis=0, keepdims=True)
        lse_ref[0, pl.ds(head, 1), :] = highest + jnp.log(total)
        return (raised * (1.0 / total)).astype(BF16)

    def mix(head, probs_low):
        at = head * head_dim
        value = heads_ref[pl.ds(2 * channels + at, head_dim), :]
        mixed_ref[pl.ds(at, head_dim), :] = nn(value, probs_low).astype(BF16)

    staged(HEADS, 2, score, soften, mix)
    attn = nn(proj_ref[...], mixed_ref[...]).astype(BF16)
    normed2, inverse2 = norm_stats(x + attn.astype(F32))
    normed2_ref[...] = normed2
    inv2_ref[...] = inverse2
    act2_ref[...] = (normed2 * column(gain2_ref[...], 2)).astype(BF16)


def forward(totals, place, x_win, qkv_weight, proj_weight, gain1, gain2):
    tokens, channels = x_win.shape
    window = WIN * WIN
    windows = tokens // window
    whole = lambda shape: pl.BlockSpec(shape, lambda w: (0,) * len(shape))
    feature = lambda rows: pl.BlockSpec((rows, window), lambda w: (0, w))
    return pl.pallas_call(
        functools.partial(forward_kernel, totals),
        grid=(windows,),
        in_specs=[
            pl.BlockSpec(memory_space=pltpu.SMEM),
            pl.BlockSpec((window, channels), lambda w: (w, 0)),
            whole(qkv_weight.shape),
            whole(proj_weight.shape),
            whole((1, channels)),
            whole((1, channels)),
        ],
        out_specs=[
            feature(3 * channels),
            feature(channels),
            feature(channels),
            feature(channels),
            feature(1),
            pl.BlockSpec((1, HEADS, window), lambda w: (w, 0, 0)),
            feature(channels),
            feature(1),
            feature(channels),
        ],
        out_shape=[
            jax.ShapeDtypeStruct((3 * channels, tokens), BF16),
            jax.ShapeDtypeStruct((channels, tokens), BF16),
            jax.ShapeDtypeStruct((channels, tokens), BF16),
            jax.ShapeDtypeStruct((channels, tokens), F32),
            jax.ShapeDtypeStruct((1, tokens), F32),
            jax.ShapeDtypeStruct((windows, HEADS, window), F32),
            jax.ShapeDtypeStruct((channels, tokens), F32),
            jax.ShapeDtypeStruct((1, tokens), F32),
            jax.ShapeDtypeStruct((channels, tokens), BF16),
        ],
        scratch_shapes=[pltpu.VMEM((window, window), F32)],
        compiler_params=pltpu.CompilerParams(vmem_limit_bytes=60 * 2**20),
        name="attention_forward",
    )(place, x_win, qkv_weight, proj_weight, gain1[None, :], gain2[None, :])


def feed_forward_kernel(
    core_ref, g_ref, act2_ref, gain2_ref, fc1_ref, fc2_ref,
    mine_ref, other_ref, grad_act2_ref, gain_ref,
    g_t_ref, fc2_sum_ref, active_ref, grad_hidden_ref,
):
    step = pl.program_id(0)
    core = core_ref[0]
    channels, tokens = act2_ref.shape
    chunk = fc1_ref.shape[0]
    rows = 32
    piece = 256

    @pl.when(step == 0)
    def _():
        g_t_ref[...] = g_ref[...].astype(F32).T.astype(BF16)
        grad_act2_ref[...] = jnp.zeros_like(grad_act2_ref)
        gain_ref[...] = jnp.zeros_like(gain_ref)

    def project(index):
        span = pl.ds(index * piece, piece)
        return nn(fc1_ref[...], act2_ref[:, span]), tn(fc2_ref[...], g_t_ref[:, span])

    def bend(index, pair):
        span = pl.ds(index * piece, piece)
        hidden, grad_active = pair
        grad_active = grad_active.astype(BF16).astype(F32)
        bell = 0.5 * (1.0 + lax.erf(hidden * ROOT_HALF))
        slope = bell + hidden * INV_ROOT_TAU * jnp.exp(-0.5 * hidden * hidden)
        grad_hidden = (grad_active * slope).astype(BF16)
        active_ref[:, span] = (hidden * bell).astype(BF16)
        grad_hidden_ref[:, span] = grad_hidden
        return grad_hidden

    def back(index, grad_hidden):
        grad_act2_ref[:, pl.ds(index * piece, piece)] += tn(fc1_ref[...], grad_hidden)

    staged(tokens // piece, 1, project, bend, back)
    fc1_part = nt(grad_hidden_ref[...], act2_ref[...])
    gain_ref[...] += jnp.sum(
        fc1_part * fc1_ref[...].astype(F32), axis=0, keepdims=True
    ) / gain2_ref[...]
    fc1_low = fc1_part.astype(BF16)
    fc2_sum_ref[step] = nt(g_t_ref[...], active_ref[...])

    def emit_fc1(place):
        for group in range(chunk // 16):
            at = step * (chunk // 32 * rows) + (group // 2) * rows
            to = pl.ds(pl.multiple_of(at, rows), 16)
            ref = mine_ref if group % 2 == place else other_ref
            ref[to, :] = fc1_low[group * 16 : (group + 1) * 16]

    by_place(core, emit_fc1)

    def emit_fc2(place):
        @pl.loop(0, channels // 8)
        def _(pair):
            at = pl.ds(pl.multiple_of(pair * 8, 8), 8)
            taken = [fc2_sum_ref[s, at, :] for s in range(4)]
            to = pl.ds(pl.multiple_of(pair * rows + 16, 16), 16)
            for half in range(2):
                block = jnp.concatenate([t[4 * half : 4 * half + 4] for t in taken], axis=0)
                ref = mine_ref if half == place else other_ref
                ref[to, :] = block.astype(BF16)

    @pl.when(step == pl.num_programs(0) - 1)
    def _():
        by_place(core, emit_fc2)


def feed_forward(core, g_win, act2, gain2, fc1_weight, fc2_weight):
    tokens, channels = g_win.shape
    hidden = fc1_weight.shape[0]
    chunk = hidden // 4
    whole = lambda shape: pl.BlockSpec(shape, lambda s: (0,) * len(shape))
    return pl.pallas_call(
        feed_forward_kernel,
        grid=(hidden // chunk,),
        in_specs=[
            pl.BlockSpec(memory_space=pltpu.SMEM),
            whole((tokens, channels)),
            whole((channels, tokens)),
            whole((1, channels)),
            pl.BlockSpec((chunk, channels), lambda s: (s, 0)),
            pl.BlockSpec((channels, chunk), lambda s: (0, s)),
        ],
        out_specs=[
            whole((hidden, channels)),
            whole((hidden, channels)),
            whole((channels, tokens)),
            whole((1, channels)),
        ],
        out_shape=[
            jax.ShapeDtypeStruct((hidden, channels), BF16),
            jax.ShapeDtypeStruct((hidden, channels), BF16),
            jax.ShapeDtypeStruct((channels, tokens), F32),
            jax.ShapeDtypeStruct((1, channels), F32),
        ],
        scratch_shapes=[
            pltpu.VMEM((channels, tokens), BF16),
            pltpu.VMEM((hidden // chunk, channels, chunk), F32),
            pltpu.VMEM((chunk, tokens), BF16),
            pltpu.VMEM((chunk, tokens), BF16),
        ],
        compiler_params=pltpu.CompilerParams(vmem_limit_bytes=60 * 2**20),
        name="feed_forward",
    )(core, g_win, act2, gain2[None, :], fc1_weight, fc2_weight)


def backward_kernel(
    totals, place_ref, g_ref, grad_act2_ref, normed2_ref, inv2_ref, heads_ref, mixed_ref, lse_ref, act1_ref,
    normed1_ref, inv1_ref, gain1_ref, gain2_ref, gain2_sum_ref, qkv_ref, proj_ref,
    dx_ref, mine_ref, other_ref,
    mask_ref, grad_mixed_ref, grad_heads_ref, qkv_sum_ref, proj_sum_ref, qkv_t_ref, proj_t_ref, gains_ref,
):
    step = pl.program_id(0)
    channels = grad_act2_ref.shape[0]
    head_dim = channels // HEADS

    @pl.when(step == 0)
    def _():
        qkv_sum_ref[...] = jnp.zeros_like(qkv_sum_ref)
        proj_sum_ref[...] = jnp.zeros_like(proj_sum_ref)
        qkv_t_ref[...] = qkv_ref[...].T
        proj_t_ref[...] = proj_ref[...].T

    mask_ref[...] = same_region(place_ref, step, totals)
    resid = g_ref[...].astype(F32).T + norm_back(
        grad_act2_ref[...] * column(gain2_ref[...], 2), normed2_ref[...], inv2_ref[...]
    )
    low = resid.astype(BF16)
    grad_mixed_ref[...] = nn(proj_t_ref[...], low).astype(BF16)
    proj_sum_ref[...] += nt(low, mixed_ref[...])

    def spans(head):
        at = head * head_dim
        return [pl.ds(group * channels + at, head_dim) for group in range(3)]

    def score(head):
        q, k, v = spans(head)
        return (
            tn(heads_ref[k, :], heads_ref[q, :]),
            tn(heads_ref[v, :], grad_mixed_ref[q, :]),
        )

    def soften(head, pair):
        scores, grad_probs = pair
        scores = jnp.where(mask_ref[...] > 0.5, scores, MASKED)
        probs = jnp.exp(scores - lse_ref[0, pl.ds(head, 1), :])
        cross = jnp.sum(probs * grad_probs, axis=0, keepdims=True)
        return probs.astype(BF16), (probs * (grad_probs - cross)).astype(BF16)

    def mix(head, pair):
        probs_low, scores_low = pair
        q, k, v = spans(head)
        grad_heads_ref[v, :] = nt(grad_mixed_ref[q, :], probs_low).astype(BF16)
        grad_heads_ref[q, :] = (nn(heads_ref[k, :], scores_low) * (head_dim ** (-0.5))).astype(BF16)
        grad_heads_ref[k, :] = nt(heads_ref[q, :], scores_low).astype(BF16)

    staged(HEADS, 1, score, soften, mix)
    grad_act1 = nn(qkv_t_ref[...], grad_heads_ref[...]).astype(BF16).astype(F32)
    qkv_sum_ref[...] += nt(grad_heads_ref[...], act1_ref[...])
    dx = resid + norm_back(grad_act1 * column(gain1_ref[...], 2), normed1_ref[...], inv1_ref[...])
    dx_ref[...] = dx.T.astype(BF16)

    def emit(place):
        @pl.loop(0, channels // 8)
        def _(pair):
            at = pl.ds(pl.multiple_of(pair * 8, 8), 8)
            qkv = qkv_sum_ref[pl.ds(pl.multiple_of(pair * 24, 8), 24), :]
            proj = proj_sum_ref[at, :]
            gain = gains_ref[at, :]
            to = pl.ds(pl.multiple_of(pair * 16, 16), 16)
            for half in range(2):
                ref = mine_ref if half == place else other_ref
                four = slice(4 * half, 4 * half + 4)
                block = jnp.concatenate([qkv[12 * half : 12 * half + 12], proj[four]], axis=0)
                ref[to, pl.ds(0, channels)] = block.astype(BF16)
                side = jnp.concatenate([jnp.zeros((12, 128), F32), gain[four]], axis=0)
                ref[to, pl.ds(channels, 128)] = side.astype(BF16)

    @pl.when(step == pl.num_programs(0) - 1)
    def _():
        gain1_sum = jnp.sum(
            qkv_sum_ref[...] * qkv_ref[...].astype(F32), axis=0, keepdims=True
        ) / gain1_ref[...]
        lines = lax.broadcasted_iota(jnp.int32, (128, channels), 0)
        gains_ref[...] = jnp.where(
            lines == 0, gain1_sum, jnp.where(lines == 1, gain2_sum_ref[...], 0.0)
        ).T
        by_place(place_ref[0], emit)


def backward(
    totals, place, g_win, grad_act2, normed2, inv2, heads, mixed, lse, act1, normed1, inv1,
    gain1, gain2, gain2_sum, qkv_weight, proj_weight,
):
    channels, tokens = grad_act2.shape
    window = WIN * WIN
    windows = tokens // window
    whole = lambda shape: pl.BlockSpec(shape, lambda w: (0,) * len(shape))
    feature = lambda rows: pl.BlockSpec((rows, window), lambda w: (0, w))
    packed = (2 * channels, channels + 128)
    return pl.pallas_call(
        functools.partial(backward_kernel, totals),
        grid=(windows,),
        in_specs=[
            pl.BlockSpec(memory_space=pltpu.SMEM),
            pl.BlockSpec((window, channels), lambda w: (w, 0)),
            feature(channels),
            feature(channels),
            feature(1),
            feature(3 * channels),
            feature(channels),
            pl.BlockSpec((1, HEADS, window), lambda w: (w, 0, 0)),
            feature(channels),
            feature(channels),
            feature(1),
            whole((1, channels)),
            whole((1, channels)),
            whole((1, channels)),
            whole(qkv_weight.shape),
            whole(proj_weight.shape),
        ],
        out_specs=[
            pl.BlockSpec((window, channels), lambda w: (w, 0)),
            whole(packed),
            whole(packed),
        ],
        out_shape=[
            jax.ShapeDtypeStruct((tokens, channels), BF16),
            jax.ShapeDtypeStruct(packed, BF16),
            jax.ShapeDtypeStruct(packed, BF16),
        ],
        scratch_shapes=[
            pltpu.VMEM((window, window), F32),
            pltpu.VMEM((channels, window), BF16),
            pltpu.VMEM((3 * channels, window), BF16),
            pltpu.VMEM((3 * channels, channels), F32),
            pltpu.VMEM((channels, channels), F32),
            pltpu.VMEM((channels, 3 * channels), BF16),
            pltpu.VMEM((channels, channels), BF16),
            pltpu.VMEM((channels, 128), F32),
        ],
        compiler_params=pltpu.CompilerParams(vmem_limit_bytes=60 * 2**20),
        cost_estimate=pl.CostEstimate(
            flops=30 * tokens * channels * window,
            bytes_accessed=20 * tokens * channels,
            transcendentals=HEADS * tokens * window,
        ),
        name="attention_backward",
    )(
        place, g_win, grad_act2, normed2, inv2, heads, mixed, lse, act1, normed1, inv1,
        gain1[None, :], gain2[None, :], gain2_sum, qkv_weight, proj_weight,
    )


def unpack_kernel(factor, pieces_ref, qkv_out_ref, proj_out_ref, gain1_out_ref, gain2_out_ref):
    rows = qkv_out_ref.shape[0]
    channels = qkv_out_ref.shape[1]
    total = pieces_ref[0].astype(F32)
    for piece in range(1, pieces_ref.shape[0]):
        total += pieces_ref[piece].astype(F32)
    total = total * factor
    qkv_out_ref[...] = total[:rows, :channels]
    proj_out_ref[...] = total[rows:, :channels]
    gains = jnp.concatenate([total[:, channels:]] * 8, axis=0).T
    gain1_out_ref[...] = gains[0:1, rows : total.shape[0]]
    gain2_out_ref[...] = gains[1:2, rows : total.shape[0]]


def unpack(pieces, rows, factor):
    channels = pieces.shape[2] - 128
    rest = pieces.shape[1] - rows
    shapes = [(rows, channels), (rest, channels), (1, rest), (1, rest)]
    return pl.pallas_call(
        functools.partial(unpack_kernel, factor),
        out_shape=[jax.ShapeDtypeStruct(shape, F32) for shape in shapes],
        compiler_params=pltpu.CompilerParams(vmem_limit_bytes=60 * 2**20),
        name="unpack",
    )(pieces)


def diagonal(block, distance):
    rows = lax.axis_size("zl") * lax.axis_size("y")
    cols = lax.axis_size("zh") * lax.axis_size("x") * lax.axis_size("core")
    route = [
        ((r - distance) % rows * cols + (c - distance) % cols, r * cols + c) for r in range(rows) for c in range(cols)
    ]
    return lax.ppermute(block, ALL, route)


def roll_in(grid, beside, below, corner):
    left = jnp.concatenate([grid[SHIFT:, SHIFT:], below], axis=0)
    right = jnp.concatenate([beside[SHIFT:], corner], axis=0)
    return jnp.concatenate([left, right], axis=1).reshape(-1, grid.shape[2])


def roll_out(grid):
    before = ring(grid[:-SHIFT, -SHIFT:], COLS, 1)
    above = ring(grid[-SHIFT:, :-SHIFT], ROWS, 1)
    corner = diagonal(grid[-SHIFT:, -SHIFT:], 1)
    top = jnp.concatenate([corner, above], axis=1)
    rest = jnp.concatenate([before, grid[:-SHIFT, :-SHIFT]], axis=1)
    return jnp.concatenate([top, rest], axis=0)


def core_sum(mine, other):
    got = lax.ppermute(other, "core", [(0, 1), (1, 0)])
    return (mine.astype(F32) + got.astype(F32)).astype(BF16)


def chips_exchange(part):
    chips = 1
    for axis in CHIPS:
        chips *= lax.axis_size(axis)
    return lax.all_to_all(part.reshape(chips, -1, part.shape[1]), CHIPS, 0, 0, tiled=True)


def shards(tokens, cotangent, gain1, qkv_weight, proj_weight, gain2, fc1_weight, fc2_weight):
    tile_rows, tile_cols, channels = tokens.shape
    devices = 1
    for axis in ALL:
        devices *= lax.axis_size(axis)
    rows_total = tile_rows * lax.axis_size("zl") * lax.axis_size("y")
    cols_total = tile_cols * (devices * tile_rows // rows_total)
    totals = (rows_total, cols_total)
    place = jnp.stack(
        [
            lax.axis_index("core"),
            lax.axis_index(ROWS) * tile_rows,
            lax.axis_index(COLS) * tile_cols,
        ]
    ).astype(jnp.int32)
    x_beside = ring(tokens[:, :SHIFT], COLS, -1)
    below = ring(jnp.stack([tokens[:SHIFT, SHIFT:], cotangent[:SHIFT, SHIFT:]]), ROWS, -1)
    corner = diagonal(jnp.stack([tokens[:SHIFT, :SHIFT], cotangent[:SHIFT, :SHIFT]]), -1)
    x_win = roll_in(tokens, x_beside, below[0], corner[0])
    g_columns, x_win = lax.optimization_barrier((cotangent[:, :SHIFT], x_win))
    g_win = roll_in(cotangent, ring(g_columns, COLS, -1), below[1], corner[1])
    heads, mixed, act1, normed1, inv1, lse, normed2, inv2, act2 = forward(
        totals, place, x_win, qkv_weight, proj_weight, gain1, gain2
    )
    ffn_mine, ffn_other, grad_act2, gain2_sum = feed_forward(
        place, g_win, act2, gain2, fc1_weight, fc2_weight
    )
    ffn_chip = core_sum(ffn_mine, ffn_other)
    grad_act2, ffn_chip = lax.optimization_barrier((grad_act2, ffn_chip))
    ffn = chips_exchange(ffn_chip).astype(F32).sum(0)
    dx, att_mine, att_other = backward(
        totals, place, g_win, grad_act2, normed2, inv2, heads, mixed, lse, act1, normed1, inv1,
        gain1, gain2, gain2_sum, qkv_weight, proj_weight,
    )
    att_chip = core_sum(att_mine, att_other)
    norm_factor = (rows_total * cols_total) ** (-0.5)
    qkv_rows = qkv_weight.shape[0] // devices
    qkv_out, proj_out, gain1_out, gain2_out = unpack(
        chips_exchange(att_chip), qkv_rows, norm_factor
    )
    grad_tokens = roll_out(dx.reshape(tile_rows, tile_cols, channels))
    ffn = ffn * norm_factor
    fc1_rows = fc1_weight.shape[0] // devices
    return (
        grad_tokens,
        qkv_out,
        proj_out,
        ffn[:fc1_rows],
        ffn[fc1_rows:].reshape(4, 4, channels).transpose(1, 0, 2).reshape(4, -1),
        gain1_out.reshape(-1),
        gain2_out.reshape(-1),
    )


def solution(mesh):
    fine = Mesh(mesh.devices.reshape(2, 4, 2, 4, 2), ALL)
    return jax.shard_map(
        shards,
        mesh=fine,
        in_specs=(P(ROWS, COLS, None), P(ROWS, COLS, None), P(), P(), P(), P(), P(), P()),
        out_specs=(
            P(ROWS, COLS, None),
            P(ALL, None),
            P(ALL, None),
            P(ALL, None),
            P(ALL, None),
            P(ALL),
            P(ALL),
        ),
        check_vma=False,
    )
```

```python
import functools

import jax
import jax.numpy as jnp
from jax import lax
from jax.experimental import pallas as pl
from jax.experimental.pallas import tpu as pltpu
from jax.sharding import Mesh, PartitionSpec as P

HEADS = 16
WIN = 16
SHIFT = 8

EPS = 1e-05
MASKED = -1000000000.0
ROOT_HALF = 0.7071067811865476
INV_ROOT_TAU = 0.3989422804014327

F32 = jnp.float32
BF16 = jnp.bfloat16
ROWS = ("zl", "y")
COLS = ("zh", "x", "core")
CHIPS = ("zl", "y", "zh", "x")
ALL = ROWS + COLS


def nn(a, b):
    return lax.dot_general(a, b, (((1,), (0,)), ((), ())), preferred_element_type=F32)


def nt(a, b):
    return lax.dot_general(a, b, (((1,), (1,)), ((), ())), preferred_element_type=F32)


def tn(a, b):
    return lax.dot_general(a, b, (((0,), (0,)), ((), ())), preferred_element_type=F32)


def ring(block, axes, distance):
    size = 1
    for axis in axes:
        size *= lax.axis_size(axis)
    route = [((i - distance) % size, i) for i in range(size)]
    return lax.ppermute(block, axes, route)


def norm_stats(values):
    average = jnp.mean(values, axis=0, keepdims=True)
    centred = values - average
    variance = jnp.mean(centred * centred, axis=0, keepdims=True)
    inverse = lax.rsqrt(variance + EPS)
    return centred * inverse, inverse


def norm_back(grad_normed, normed, inverse):
    mean_grad = jnp.mean(grad_normed, axis=0, keepdims=True)
    mean_cross = jnp.mean(grad_normed * normed, axis=0, keepdims=True)
    return (grad_normed - mean_grad - normed * mean_cross) * inverse


def staged(count, lead, first, second, third):
    opened, closed = {}, {}
    for turn in range(count + lead + 1):
        if turn < count:
            opened[turn] = first(turn)
        if 0 <= turn - lead < count:
            closed[turn - lead] = second(turn - lead, opened.pop(turn - lead))
        if 0 <= turn - lead - 1 < count:
            third(turn - lead - 1, closed.pop(turn - lead - 1))


def by_place(core, emit):
    for place in range(2):

        @pl.when(core == place)
        def _():
            emit(place)


def region(coords, total):
    return jnp.where(coords < total - WIN, 0, jnp.where(coords < total - SHIFT, 1, 2)).astype(
        jnp.int32
    )


def column(row, copies):
    block = jnp.broadcast_to(row, (128, row.shape[1])).T
    return jnp.concatenate([block] * copies, axis=1)


def same_region(place_ref, window, totals):
    def labels(shape, dim):
        token = lax.broadcasted_iota(jnp.int32, shape, dim)
        down = place_ref[1] + window * WIN + token // WIN
        along = place_ref[2] + token % WIN
        return 3 * region(down, totals[0]) + region(along, totals[1])

    tokens = WIN * WIN
    return (labels((tokens, tokens), 0) == labels((tokens, tokens), 1)).astype(F32)


def forward_kernel(
    totals, place_ref, x_ref, qkv_ref, proj_ref, gain1_ref, gain2_ref,
    heads_ref, mixed_ref, act1_ref, normed1_ref, inv1_ref, lse_ref, normed2_ref, inv2_ref, act2_ref,
    mask_ref,
):
    channels = x_ref.shape[1]
    head_dim = channels // HEADS
    x = x_ref[...].astype(F32).T
    normed1, inverse1 = norm_stats(x)
    act1 = (normed1 * column(gain1_ref[...], 2)).astype(BF16)
    act1_ref[...] = act1
    normed1_ref[...] = normed1
    inv1_ref[...] = inverse1
    queries = nn(qkv_ref[pl.ds(0, channels), :], act1) * (head_dim ** (-0.5))
    heads_ref[pl.ds(0, channels), :] = queries.astype(BF16)
    heads_ref[pl.ds(channels, 2 * channels), :] = nn(
        qkv_ref[pl.ds(channels, 2 * channels), :], act1
    ).astype(BF16)
    mask_ref[...] = same_region(place_ref, pl.program_id(0), totals)

    def score(head):
        at = head * head_dim
        return tn(heads_ref[pl.ds(channels + at, head_dim), :], heads_ref[pl.ds(at, head_dim), :])

    def soften(head, scores):
        scores = jnp.where(mask_ref[...] > 0.5, scores, MASKED)
        highest = jnp.max(scores, axis=0, keepdims=True)
        raised = jnp.exp(scores - highest)
        total = jnp.sum(raised, axis=0, keepdims=True)
        lse_ref[0, pl.ds(head, 1), :] = highest + jnp.log(total)
        return (raised * (1.0 / total)).astype(BF16)

    def mix(head, probs_low):
        at = head * head_dim
        value = heads_ref[pl.ds(2 * channels + at, head_dim), :]
        mixed_ref[pl.ds(at, head_dim), :] = nn(value, probs_low).astype(BF16)

    staged(HEADS, 2, score, soften, mix)
    attn = nn(proj_ref[...], mixed_ref[...]).astype(BF16)
    normed2, inverse2 = norm_stats(x + attn.astype(F32))
    normed2_ref[...] = normed2
    inv2_ref[...] = inverse2
    act2_ref[...] = (normed2 * column(gain2_ref[...], 2)).astype(BF16)


def forward(totals, place, x_win, qkv_weight, proj_weight, gain1, gain2):
    tokens, channels = x_win.shape
    window = WIN * WIN
    windows = tokens // window
    whole = lambda shape: pl.BlockSpec(shape, lambda w: (0,) * len(shape))
    feature = lambda rows: pl.BlockSpec((rows, window), lambda w: (0, w))
    return pl.pallas_call(
        functools.partial(forward_kernel, totals),
        grid=(windows,),
        in_specs=[
            pl.BlockSpec(memory_space=pltpu.SMEM),
            pl.BlockSpec((window, channels), lambda w: (w, 0)),
            whole(qkv_weight.shape),
            whole(proj_weight.shape),
            whole((1, channels)),
            whole((1, channels)),
        ],
        out_specs=[
            feature(3 * channels),
            feature(channels),
            feature(channels),
            feature(channels),
            feature(1),
            pl.BlockSpec((1, HEADS, window), lambda w: (w, 0, 0)),
            feature(channels),
            feature(1),
            feature(channels),
        ],
        out_shape=[
            jax.ShapeDtypeStruct((3 * channels, tokens), BF16),
            jax.ShapeDtypeStruct((channels, tokens), BF16),
            jax.ShapeDtypeStruct((channels, tokens), BF16),
            jax.ShapeDtypeStruct((channels, tokens), F32),
            jax.ShapeDtypeStruct((1, tokens), F32),
            jax.ShapeDtypeStruct((windows, HEADS, window), F32),
            jax.ShapeDtypeStruct((channels, tokens), F32),
            jax.ShapeDtypeStruct((1, tokens), F32),
            jax.ShapeDtypeStruct((channels, tokens), BF16),
        ],
        scratch_shapes=[pltpu.VMEM((window, window), F32)],
        compiler_params=pltpu.CompilerParams(vmem_limit_bytes=60 * 2**20),
        name="attention_forward",
    )(place, x_win, qkv_weight, proj_weight, gain1[None, :], gain2[None, :])


def feed_forward_kernel(
    core_ref, g_ref, act2_ref, gain2_ref, fc1_ref, fc2_ref,
    mine_ref, other_ref, grad_act2_ref, gain_ref,
    g_t_ref, fc2_sum_ref, active_ref, grad_hidden_ref,
):
    step = pl.program_id(0)
    core = core_ref[0]
    channels, tokens = act2_ref.shape
    chunk = fc1_ref.shape[0]
    rows = 32
    piece = 256

    @pl.when(step == 0)
    def _():
        g_t_ref[...] = g_ref[...].astype(F32).T.astype(BF16)
        grad_act2_ref[...] = jnp.zeros_like(grad_act2_ref)
        gain_ref[...] = jnp.zeros_like(gain_ref)

    def project(index):
        span = pl.ds(index * piece, piece)
        return nn(fc1_ref[...], act2_ref[:, span]), tn(fc2_ref[...], g_t_ref[:, span])

    def bend(index, pair):
        span = pl.ds(index * piece, piece)
        hidden, grad_active = pair
        grad_active = grad_active.astype(BF16).astype(F32)
        bell = 0.5 * (1.0 + lax.erf(hidden * ROOT_HALF))
        slope = bell + hidden * INV_ROOT_TAU * jnp.exp(-0.5 * hidden * hidden)
        grad_hidden = (grad_active * slope).astype(BF16)
        active_ref[:, span] = (hidden * bell).astype(BF16)
        grad_hidden_ref[:, span] = grad_hidden
        return grad_hidden

    def back(index, grad_hidden):
        grad_act2_ref[:, pl.ds(index * piece, piece)] += tn(fc1_ref[...], grad_hidden)

    staged(tokens // piece, 1, project, bend, back)
    fc1_part = nt(grad_hidden_ref[...], act2_ref[...])
    gain_ref[...] += jnp.sum(
        fc1_part * fc1_ref[...].astype(F32), axis=0, keepdims=True
    ) / gain2_ref[...]
    fc1_low = fc1_part.astype(BF16)
    fc2_sum_ref[step] = nt(g_t_ref[...], active_ref[...])

    def emit_fc1(place):
        for group in range(chunk // 16):
            at = step * (chunk // 32 * rows) + (group // 2) * rows
            to = pl.ds(pl.multiple_of(at, rows), 16)
            ref = mine_ref if group % 2 == place else other_ref
            ref[to, :] = fc1_low[group * 16 : (group + 1) * 16]

    by_place(core, emit_fc1)

    def emit_fc2(place):
        @pl.loop(0, channels // 8)
        def _(pair):
            at = pl.ds(pl.multiple_of(pair * 8, 8), 8)
            taken = [fc2_sum_ref[s, at, :] for s in range(4)]
            to = pl.ds(pl.multiple_of(pair * rows + 16, 16), 16)
            for half in range(2):
                block = jnp.concatenate([t[4 * half : 4 * half + 4] for t in taken], axis=0)
                ref = mine_ref if half == place else other_ref
                ref[to, :] = block.astype(BF16)

    @pl.when(step == pl.num_programs(0) - 1)
    def _():
        by_place(core, emit_fc2)


def feed_forward(core, g_win, act2, gain2, fc1_weight, fc2_weight):
    tokens, channels = g_win.shape
    hidden = fc1_weight.shape[0]
    chunk = hidden // 4
    whole = lambda shape: pl.BlockSpec(shape, lambda s: (0,) * len(shape))
    return pl.pallas_call(
        feed_forward_kernel,
        grid=(hidden // chunk,),
        in_specs=[
            pl.BlockSpec(memory_space=pltpu.SMEM),
            whole((tokens, channels)),
            whole((channels, tokens)),
            whole((1, channels)),
            pl.BlockSpec((chunk, channels), lambda s: (s, 0)),
            pl.BlockSpec((channels, chunk), lambda s: (0, s)),
        ],
        out_specs=[
            whole((hidden, channels)),
            whole((hidden, channels)),
            whole((channels, tokens)),
            whole((1, channels)),
        ],
        out_shape=[
            jax.ShapeDtypeStruct((hidden, channels), BF16),
            jax.ShapeDtypeStruct((hidden, channels), BF16),
            jax.ShapeDtypeStruct((channels, tokens), F32),
            jax.ShapeDtypeStruct((1, channels), F32),
        ],
        scratch_shapes=[
            pltpu.VMEM((channels, tokens), BF16),
            pltpu.VMEM((hidden // chunk, channels, chunk), F32),
            pltpu.VMEM((chunk, tokens), BF16),
            pltpu.VMEM((chunk, tokens), BF16),
        ],
        compiler_params=pltpu.CompilerParams(vmem_limit_bytes=60 * 2**20),
        name="feed_forward",
    )(core, g_win, act2, gain2[None, :], fc1_weight, fc2_weight)


def backward_kernel(
    totals, place_ref, g_ref, grad_act2_ref, normed2_ref, inv2_ref, heads_ref, mixed_ref, lse_ref, act1_ref,
    normed1_ref, inv1_ref, gain1_ref, gain2_ref, gain2_sum_ref, qkv_ref, proj_ref,
    dx_left_ref, dx_right_ref, mine_ref, other_ref,
    mask_ref, grad_mixed_ref, grad_heads_ref, qkv_sum_ref, proj_sum_ref, qkv_t_ref, proj_t_ref, gains_ref,
):
    step = pl.program_id(0)
    channels = grad_act2_ref.shape[0]
    head_dim = channels // HEADS

    @pl.when(step == 0)
    def _():
        qkv_sum_ref[...] = jnp.zeros_like(qkv_sum_ref)
        proj_sum_ref[...] = jnp.zeros_like(proj_sum_ref)
        qkv_t_ref[...] = qkv_ref[...].T
        proj_t_ref[...] = proj_ref[...].T

    mask_ref[...] = same_region(place_ref, step, totals)
    resid = g_ref[...].astype(F32).T + norm_back(
        grad_act2_ref[...] * column(gain2_ref[...], 2), normed2_ref[...], inv2_ref[...]
    )
    low = resid.astype(BF16)
    grad_mixed_ref[...] = nn(proj_t_ref[...], low).astype(BF16)
    proj_sum_ref[...] += nt(low, mixed_ref[...])

    def spans(head):
        at = head * head_dim
        return [pl.ds(group * channels + at, head_dim) for group in range(3)]

    def score(head):
        q, k, v = spans(head)
        return (
            tn(heads_ref[k, :], heads_ref[q, :]),
            tn(heads_ref[v, :], grad_mixed_ref[q, :]),
        )

    def soften(head, pair):
        scores, grad_probs = pair
        scores = jnp.where(mask_ref[...] > 0.5, scores, MASKED)
        probs = jnp.exp(scores - lse_ref[0, pl.ds(head, 1), :])
        cross = jnp.sum(probs * grad_probs, axis=0, keepdims=True)
        return probs.astype(BF16), (probs * (grad_probs - cross)).astype(BF16)

    def mix(head, pair):
        probs_low, scores_low = pair
        q, k, v = spans(head)
        grad_heads_ref[v, :] = nt(grad_mixed_ref[q, :], probs_low).astype(BF16)
        grad_heads_ref[q, :] = (nn(heads_ref[k, :], scores_low) * (head_dim ** (-0.5))).astype(BF16)
        grad_heads_ref[k, :] = nt(heads_ref[q, :], scores_low).astype(BF16)

    staged(HEADS, 1, score, soften, mix)
    grad_act1 = nn(qkv_t_ref[...], grad_heads_ref[...]).astype(BF16).astype(F32)
    qkv_sum_ref[...] += nt(grad_heads_ref[...], act1_ref[...])
    dx = resid + norm_back(grad_act1 * column(gain1_ref[...], 2), normed1_ref[...], inv1_ref[...])
    dx = dx.T.reshape(WIN, WIN, channels)
    dx_left_ref[...] = dx[:, :SHIFT].reshape(-1, channels).astype(BF16)
    dx_right_ref[...] = dx[:, SHIFT:].reshape(-1, channels).astype(BF16)

    def emit(place):
        @pl.loop(0, channels // 8)
        def _(pair):
            at = pl.ds(pl.multiple_of(pair * 8, 8), 8)
            qkv = qkv_sum_ref[pl.ds(pl.multiple_of(pair * 24, 8), 24), :]
            proj = proj_sum_ref[at, :]
            gain = gains_ref[at, :]
            to = pl.ds(pl.multiple_of(pair * 16, 16), 16)
            for half in range(2):
                ref = mine_ref if half == place else other_ref
                four = slice(4 * half, 4 * half + 4)
                block = jnp.concatenate([qkv[12 * half : 12 * half + 12], proj[four]], axis=0)
                ref[to, pl.ds(0, channels)] = block.astype(BF16)
                side = jnp.concatenate([jnp.zeros((12, 128), F32), gain[four]], axis=0)
                ref[to, pl.ds(channels, 128)] = side.astype(BF16)

    @pl.when(step == pl.num_programs(0) - 1)
    def _():
        gain1_sum = jnp.sum(
            qkv_sum_ref[...] * qkv_ref[...].astype(F32), axis=0, keepdims=True
        ) / gain1_ref[...]
        lines = lax.broadcasted_iota(jnp.int32, (128, channels), 0)
        gains_ref[...] = jnp.where(
            lines == 0, gain1_sum, jnp.where(lines == 1, gain2_sum_ref[...], 0.0)
        ).T
        by_place(place_ref[0], emit)


def backward(
    totals, place, g_win, grad_act2, normed2, inv2, heads, mixed, lse, act1, normed1, inv1,
    gain1, gain2, gain2_sum, qkv_weight, proj_weight,
):
    channels, tokens = grad_act2.shape
    window = WIN * WIN
    windows = tokens // window
    whole = lambda shape: pl.BlockSpec(shape, lambda w: (0,) * len(shape))
    feature = lambda rows: pl.BlockSpec((rows, window), lambda w: (0, w))
    packed = (2 * channels, channels + 128)
    return pl.pallas_call(
        functools.partial(backward_kernel, totals),
        grid=(windows,),
        in_specs=[
            pl.BlockSpec(memory_space=pltpu.SMEM),
            pl.BlockSpec((window, channels), lambda w: (w, 0)),
            feature(channels),
            feature(channels),
            feature(1),
            feature(3 * channels),
            feature(channels),
            pl.BlockSpec((1, HEADS, window), lambda w: (w, 0, 0)),
            feature(channels),
            feature(channels),
            feature(1),
            whole((1, channels)),
            whole((1, channels)),
            whole((1, channels)),
            whole(qkv_weight.shape),
            whole(proj_weight.shape),
        ],
        out_specs=[
            pl.BlockSpec((window // 2, channels), lambda w: (w, 0)),
            pl.BlockSpec((window // 2, channels), lambda w: (w, 0)),
            whole(packed),
            whole(packed),
        ],
        out_shape=[
            jax.ShapeDtypeStruct((tokens // 2, channels), BF16),
            jax.ShapeDtypeStruct((tokens // 2, channels), BF16),
            jax.ShapeDtypeStruct(packed, BF16),
            jax.ShapeDtypeStruct(packed, BF16),
        ],
        scratch_shapes=[
            pltpu.VMEM((window, window), F32),
            pltpu.VMEM((channels, window), BF16),
            pltpu.VMEM((3 * channels, window), BF16),
            pltpu.VMEM((3 * channels, channels), F32),
            pltpu.VMEM((channels, channels), F32),
            pltpu.VMEM((channels, 3 * channels), BF16),
            pltpu.VMEM((channels, channels), BF16),
            pltpu.VMEM((channels, 128), F32),
        ],
        compiler_params=pltpu.CompilerParams(vmem_limit_bytes=60 * 2**20),
        cost_estimate=pl.CostEstimate(
            flops=30 * tokens * channels * window,
            bytes_accessed=20 * tokens * channels,
            transcendentals=HEADS * tokens * window,
        ),
        name="attention_backward",
    )(
        place, g_win, grad_act2, normed2, inv2, heads, mixed, lse, act1, normed1, inv1,
        gain1[None, :], gain2[None, :], gain2_sum, qkv_weight, proj_weight,
    )


def unpack_kernel(factor, pieces_ref, qkv_out_ref, proj_out_ref, gain1_out_ref, gain2_out_ref, sum_ref):
    step = pl.program_id(0)

    @pl.when(step == 0)
    def _():
        sum_ref[...] = jnp.zeros_like(sum_ref)

    total = sum_ref[...]
    for piece in range(pieces_ref.shape[0]):
        total += pieces_ref[piece].astype(F32)
    sum_ref[...] = total

    @pl.when(step == pl.num_programs(0) - 1)
    def _():
        rows, channels = qkv_out_ref.shape
        scaled = sum_ref[...] * factor
        qkv_out_ref[...] = scaled[:rows, :channels]
        proj_out_ref[...] = scaled[rows:, :channels]
        gains = jnp.concatenate([scaled[:, channels:]] * 8, axis=0).T
        gain1_out_ref[...] = gains[0:1, rows : scaled.shape[0]]
        gain2_out_ref[...] = gains[1:2, rows : scaled.shape[0]]


def unpack(pieces, rows, factor):
    chips, both, columns = pieces.shape
    channels = columns - 128
    rest = both - rows
    shapes = [(rows, channels), (rest, channels), (1, rest), (1, rest)]
    return pl.pallas_call(
        functools.partial(unpack_kernel, factor),
        grid=(2,),
        in_specs=[pl.BlockSpec((chips // 2, both, columns), lambda s: (s, 0, 0))],
        out_specs=[pl.BlockSpec(shape, lambda s: (0, 0)) for shape in shapes],
        out_shape=[jax.ShapeDtypeStruct(shape, F32) for shape in shapes],
        scratch_shapes=[pltpu.VMEM((both, columns), F32)],
        compiler_params=pltpu.CompilerParams(vmem_limit_bytes=64 * 2**20),
        name="unpack",
    )(pieces)


def unpack_ffn_kernel(factor, pieces_ref, fc1_out_ref, fc2_out_ref, sum_ref):
    step = pl.program_id(0)

    @pl.when(step == 0)
    def _():
        sum_ref[...] = jnp.zeros_like(sum_ref)

    total = sum_ref[...]
    for piece in range(pieces_ref.shape[0]):
        total += pieces_ref[piece].astype(F32)
    sum_ref[...] = total

    @pl.when(step == pl.num_programs(0) - 1)
    def _():
        rows, channels = fc1_out_ref.shape
        scaled = sum_ref[...] * factor
        fc1_out_ref[...] = scaled[:rows]
        for part in range(fc2_out_ref.shape[1] // channels):
            at = rows + 4 * part
            fc2_out_ref[:, pl.ds(part * channels, channels)] = scaled[at : at + 4]


def unpack_ffn(pieces, fc1_rows, factor):
    chips, rows, channels = pieces.shape
    fc2_rows = (rows - fc1_rows) // 4
    shapes = [(fc1_rows, channels), (fc2_rows, 4 * channels)]
    return pl.pallas_call(
        functools.partial(unpack_ffn_kernel, factor),
        grid=(4,),
        in_specs=[pl.BlockSpec((chips // 4, rows, channels), lambda s: (s, 0, 0))],
        out_specs=[pl.BlockSpec(shape, lambda s: (0, 0)) for shape in shapes],
        out_shape=[jax.ShapeDtypeStruct(shape, F32) for shape in shapes],
        scratch_shapes=[pltpu.VMEM((rows, channels), F32)],
        compiler_params=pltpu.CompilerParams(vmem_limit_bytes=64 * 2**20),
        cost_estimate=pl.CostEstimate(
            flops=2**30, bytes_accessed=2 * chips * rows * channels, transcendentals=0
        ),
        name="unpack_ffn",
    )(pieces)


def diagonal(block, distance):
    rows = lax.axis_size("zl") * lax.axis_size("y")
    cols = lax.axis_size("zh") * lax.axis_size("x") * lax.axis_size("core")
    route = [
        ((r - distance) % rows * cols + (c - distance) % cols, r * cols + c) for r in range(rows) for c in range(cols)
    ]
    return lax.ppermute(block, ALL, route)


def roll_in(grid, beside, below, corner):
    left = jnp.concatenate([grid[SHIFT:, SHIFT:], below], axis=0)
    right = jnp.concatenate([beside, corner], axis=0)
    return jnp.concatenate([left, right], axis=1).reshape(-1, grid.shape[2])


def roll_out(left, right):
    before = ring(right, COLS, 1)[:-SHIFT]
    above = ring(left[-SHIFT:], ROWS, 1)
    corner = diagonal(right[-SHIFT:], 1)
    top = jnp.concatenate([corner, above], axis=1)
    rest = jnp.concatenate([before, left[:-SHIFT]], axis=1)
    return jnp.concatenate([top, rest], axis=0)


def core_sum(mine, other):
    got = lax.ppermute(other, "core", [(0, 1), (1, 0)])
    return (mine.astype(F32) + got.astype(F32)).astype(BF16)


def chips_exchange(part):
    chips = 1
    for axis in CHIPS:
        chips *= lax.axis_size(axis)
    return lax.all_to_all(part.reshape(chips, -1, part.shape[1]), CHIPS, 0, 0, tiled=True)


def shards(tokens, cotangent, gain1, qkv_weight, proj_weight, gain2, fc1_weight, fc2_weight):
    tile_rows, tile_cols, channels = tokens.shape
    devices = 1
    for axis in ALL:
        devices *= lax.axis_size(axis)
    rows_total = tile_rows * lax.axis_size("zl") * lax.axis_size("y")
    cols_total = tile_cols * (devices * tile_rows // rows_total)
    totals = (rows_total, cols_total)
    place = jnp.stack(
        [
            lax.axis_index("core"),
            lax.axis_index(ROWS) * tile_rows,
            lax.axis_index(COLS) * tile_cols,
        ]
    ).astype(jnp.int32)
    first = jnp.stack([tokens[:SHIFT], cotangent[:SHIFT]])
    below = ring(first[:, :, SHIFT:], ROWS, -1)
    corner = diagonal(first[:, :, :SHIFT], -1)
    x_win = roll_in(tokens, ring(tokens[SHIFT:, :SHIFT], COLS, -1), below[0], corner[0])
    g_beside = ring(cotangent[SHIFT:, :SHIFT], COLS, -1)
    heads, mixed, act1, normed1, inv1, lse, normed2, inv2, act2 = forward(
        totals, place, x_win, qkv_weight, proj_weight, gain1, gain2
    )
    act2, g_beside = lax.optimization_barrier((act2, g_beside))
    g_win = roll_in(cotangent, g_beside, below[1], corner[1])
    ffn_mine, ffn_other, grad_act2, gain2_sum = feed_forward(
        place, g_win, act2, gain2, fc1_weight, fc2_weight
    )
    ffn_chip = core_sum(ffn_mine, ffn_other)
    grad_act2, ffn_chip = lax.optimization_barrier((grad_act2, ffn_chip))
    ffn_pieces = chips_exchange(ffn_chip)
    dx_left, dx_right, att_mine, att_other = backward(
        totals, place, g_win, grad_act2, normed2, inv2, heads, mixed, lse, act1, normed1, inv1,
        gain1, gain2, gain2_sum, qkv_weight, proj_weight,
    )
    halves = (tile_rows, SHIFT, channels)
    grad_tokens = roll_out(dx_left.reshape(halves), dx_right.reshape(halves))
    att_chip = core_sum(att_mine, att_other)
    att_chip, grad_tokens = lax.optimization_barrier((att_chip, grad_tokens))
    norm_factor = (rows_total * cols_total) ** (-0.5)
    qkv_rows = qkv_weight.shape[0] // devices
    qkv_out, proj_out, gain1_out, gain2_out = unpack(
        chips_exchange(att_chip), qkv_rows, norm_factor
    )
    fc1_out, fc2_out = unpack_ffn(ffn_pieces, fc1_weight.shape[0] // devices, norm_factor)
    return (
        grad_tokens,
        qkv_out,
        proj_out,
        fc1_out,
        fc2_out,
        gain1_out.reshape(-1),
        gain2_out.reshape(-1),
    )


def solution(mesh):
    fine = Mesh(mesh.devices.reshape(2, 4, 2, 4, 2), ALL)
    return jax.shard_map(
        shards,
        mesh=fine,
        in_specs=(P(ROWS, COLS, None), P(ROWS, COLS, None), P(), P(), P(), P(), P(), P()),
        out_specs=(
            P(ROWS, COLS, None),
            P(ALL, None),
            P(ALL, None),
            P(ALL, None),
            P(ALL, None),
            P(ALL),
            P(ALL),
        ),
        check_vma=False,
    )
```

```python
import functools

import jax
import jax.numpy as jnp
from jax import lax
from jax.experimental import pallas as pl
from jax.experimental.pallas import tpu as pltpu
from jax.sharding import Mesh, PartitionSpec as P

HEADS = 16
WIN = 16
SHIFT = 8

EPS = 1e-05
MASKED = -1000000000.0
ROOT_HALF = 0.7071067811865476
INV_ROOT_TAU = 0.3989422804014327

F32 = jnp.float32
BF16 = jnp.bfloat16
ROWS = ("zl", "y")
COLS = ("zh", "x", "core")
CHIPS = ("zl", "y", "zh", "x")
ALL = ROWS + COLS


def nn(a, b):
    return lax.dot_general(a, b, (((1,), (0,)), ((), ())), preferred_element_type=F32)


def nt(a, b):
    return lax.dot_general(a, b, (((1,), (1,)), ((), ())), preferred_element_type=F32)


def tn(a, b):
    return lax.dot_general(a, b, (((0,), (0,)), ((), ())), preferred_element_type=F32)


def ring(block, axes, distance):
    size = 1
    for axis in axes:
        size *= lax.axis_size(axis)
    route = [((i - distance) % size, i) for i in range(size)]
    return lax.ppermute(block, axes, route)


def norm_stats(values):
    average = jnp.mean(values, axis=0, keepdims=True)
    centred = values - average
    variance = jnp.mean(centred * centred, axis=0, keepdims=True)
    inverse = lax.rsqrt(variance + EPS)
    return centred * inverse, inverse


def norm_back(grad_normed, normed, inverse):
    mean_grad = jnp.mean(grad_normed, axis=0, keepdims=True)
    mean_cross = jnp.mean(grad_normed * normed, axis=0, keepdims=True)
    return (grad_normed - mean_grad - normed * mean_cross) * inverse


def staged(count, lead, first, second, third):
    opened, closed = {}, {}
    for turn in range(count + lead + 1):
        if turn < count:
            opened[turn] = first(turn)
        if 0 <= turn - lead < count:
            closed[turn - lead] = second(turn - lead, opened.pop(turn - lead))
        if 0 <= turn - lead - 1 < count:
            third(turn - lead - 1, closed.pop(turn - lead - 1))


def by_place(core, emit):
    for place in range(2):

        @pl.when(core == place)
        def _():
            emit(place)


def region(coords, total):
    return jnp.where(coords < total - WIN, 0, jnp.where(coords < total - SHIFT, 1, 2)).astype(
        jnp.int32
    )


def column(row, copies):
    block = jnp.broadcast_to(row, (128, row.shape[1])).T
    return jnp.concatenate([block] * copies, axis=1)


def same_region(place_ref, window, totals):
    tokens = WIN * WIN

    def labels(shape, dim):
        token = lax.broadcasted_iota(jnp.int32, shape, dim)
        down = place_ref[1] + window * WIN + token % (tokens // 2) // SHIFT
        along = place_ref[2] + token // (tokens // 2) * SHIFT + token % SHIFT
        return 3 * region(down, totals[0]) + region(along, totals[1])

    return (labels((tokens, tokens), 0) == labels((tokens, tokens), 1)).astype(F32)


def forward_kernel(
    totals, place_ref, x_own_ref, x_own_next_ref, x_side_ref, x_side_next_ref, x_below_ref, x_corner_ref, qkv_ref, proj_ref, gain1_ref, gain2_ref,
    heads_ref, mixed_ref, act1_ref, normed1_ref, inv1_ref, lse_ref, normed2_ref, inv2_ref, act2_ref,
    mask_ref,
):
    channels = x_own_ref.shape[1]
    head_dim = channels // HEADS
    last = pl.program_id(0) == pl.num_programs(0) - 1
    pieces = [
        x_own_ref[...].astype(F32),
        jnp.where(last, x_below_ref[...].astype(F32), x_own_next_ref[...].astype(F32)),
        x_side_ref[...].astype(F32),
        jnp.where(last, x_corner_ref[...].astype(F32), x_side_next_ref[...].astype(F32)),
    ]
    x = jnp.concatenate(pieces, axis=0).T
    normed1, inverse1 = norm_stats(x)
    act1 = (normed1 * column(gain1_ref[...], 2)).astype(BF16)
    act1_ref[...] = act1
    normed1_ref[...] = normed1
    inv1_ref[...] = inverse1
    queries = nn(qkv_ref[pl.ds(0, channels), :], act1) * (head_dim ** (-0.5))
    heads_ref[pl.ds(0, channels), :] = queries.astype(BF16)
    heads_ref[pl.ds(channels, 2 * channels), :] = nn(
        qkv_ref[pl.ds(channels, 2 * channels), :], act1
    ).astype(BF16)
    mask_ref[...] = same_region(place_ref, pl.program_id(0), totals)

    def score(head):
        at = head * head_dim
        return tn(heads_ref[pl.ds(channels + at, head_dim), :], heads_ref[pl.ds(at, head_dim), :])

    def soften(head, scores):
        scores = jnp.where(mask_ref[...] > 0.5, scores, MASKED)
        highest = jnp.max(scores, axis=0, keepdims=True)
        raised = jnp.exp(scores - highest)
        total = jnp.sum(raised, axis=0, keepdims=True)
        lse_ref[0, pl.ds(head, 1), :] = highest + jnp.log(total)
        return (raised * (1.0 / total)).astype(BF16)

    def mix(head, probs_low):
        at = head * head_dim
        value = heads_ref[pl.ds(2 * channels + at, head_dim), :]
        mixed_ref[pl.ds(at, head_dim), :] = nn(value, probs_low).astype(BF16)

    staged(HEADS, 2, score, soften, mix)
    attn = nn(proj_ref[...], mixed_ref[...]).astype(BF16)
    normed2, inverse2 = norm_stats(x + attn.astype(F32))
    normed2_ref[...] = normed2
    inv2_ref[...] = inverse2
    act2_ref[...] = (normed2 * column(gain2_ref[...], 2)).astype(BF16)


def forward(totals, place, x_own, x_side, x_below, x_corner, qkv_weight, proj_weight, gain1, gain2):
    quarter, channels = x_below.shape
    tokens = 2 * (x_own.shape[0] + quarter)
    window = WIN * WIN
    windows = tokens // window
    whole = lambda shape: pl.BlockSpec(shape, lambda w: (0,) * len(shape))
    feature = lambda rows: pl.BlockSpec((rows, window), lambda w: (0, w))
    here = pl.BlockSpec((quarter, channels), lambda w: (2 * w, 0))
    following = pl.BlockSpec(
        (quarter, channels), lambda w: (jnp.minimum(2 * w + 1, 2 * windows - 2), 0)
    )
    return pl.pallas_call(
        functools.partial(forward_kernel, totals),
        grid=(windows,),
        in_specs=[
            pl.BlockSpec(memory_space=pltpu.SMEM),
            here,
            following,
            here,
            following,
            whole(x_below.shape),
            whole(x_corner.shape),
            whole(qkv_weight.shape),
            whole(proj_weight.shape),
            whole((1, channels)),
            whole((1, channels)),
        ],
        out_specs=[
            feature(3 * channels),
            feature(channels),
            feature(channels),
            feature(channels),
            feature(1),
            pl.BlockSpec((1, HEADS, window), lambda w: (w, 0, 0)),
            feature(channels),
            feature(1),
            feature(channels),
        ],
        out_shape=[
            jax.ShapeDtypeStruct((3 * channels, tokens), BF16),
            jax.ShapeDtypeStruct((channels, tokens), BF16),
            jax.ShapeDtypeStruct((channels, tokens), BF16),
            jax.ShapeDtypeStruct((channels, tokens), F32),
            jax.ShapeDtypeStruct((1, tokens), F32),
            jax.ShapeDtypeStruct((windows, HEADS, window), F32),
            jax.ShapeDtypeStruct((channels, tokens), F32),
            jax.ShapeDtypeStruct((1, tokens), F32),
            jax.ShapeDtypeStruct((channels, tokens), BF16),
        ],
        scratch_shapes=[pltpu.VMEM((window, window), F32)],
        compiler_params=pltpu.CompilerParams(vmem_limit_bytes=64 * 2**20),
        name="attention_forward",
    )(
        place, x_own, x_own, x_side, x_side, x_below, x_corner, qkv_weight, proj_weight,
        gain1[None, :], gain2[None, :],
    )


def feed_forward_kernel(
    core_ref, g_own_ref, g_side_ref, g_below_ref, g_corner_ref, act2_ref, gain2_ref, fc1_ref, fc2_ref,
    mine_ref, other_ref, grad_act2_ref, gain_ref, g_t_ref,
    fc2_sum_ref, active_ref, grad_hidden_ref,
):
    step = pl.program_id(0)
    core = core_ref[0]
    channels, tokens = act2_ref.shape
    chunk = fc1_ref.shape[0]
    rows = 32
    piece = 256

    @pl.when(step == 0)
    def _():
        half = WIN * SHIFT
        halves = [(g_own_ref, g_below_ref), (g_side_ref, g_corner_ref)]
        for window in range(tokens // (2 * half)):
            at = window * half
            pieces = []
            for ref, last_ref in halves:
                if at + half <= ref.shape[0]:
                    pieces.append(ref[pl.ds(at, half), :])
                else:
                    pieces += [ref[pl.ds(at, half // 2), :], last_ref[...]]
            joined = jnp.concatenate([piece.astype(F32) for piece in pieces], axis=0)
            g_t_ref[:, pl.ds(2 * at, 2 * half)] = joined.T.astype(BF16)
        grad_act2_ref[...] = jnp.zeros_like(grad_act2_ref)
        gain_ref[...] = jnp.zeros_like(gain_ref)

    def project(index):
        span = pl.ds(index * piece, piece)
        return nn(fc1_ref[...], act2_ref[:, span]), tn(fc2_ref[...], g_t_ref[:, span])

    def bend(index, pair):
        span = pl.ds(index * piece, piece)
        hidden, grad_active = pair
        grad_active = grad_active.astype(BF16).astype(F32)
        bell = 0.5 * (1.0 + lax.erf(hidden * ROOT_HALF))
        slope = bell + hidden * INV_ROOT_TAU * jnp.exp(-0.5 * hidden * hidden)
        grad_hidden = (grad_active * slope).astype(BF16)
        active_ref[:, span] = (hidden * bell).astype(BF16)
        grad_hidden_ref[:, span] = grad_hidden
        return grad_hidden

    def back(index, grad_hidden):
        grad_act2_ref[:, pl.ds(index * piece, piece)] += tn(fc1_ref[...], grad_hidden)

    staged(tokens // piece, 1, project, bend, back)
    fc1_part = nt(grad_hidden_ref[...], act2_ref[...])
    gain_ref[...] += jnp.sum(
        fc1_part * fc1_ref[...].astype(F32), axis=0, keepdims=True
    ) / gain2_ref[...]
    fc1_low = fc1_part.astype(BF16)
    fc2_sum_ref[step] = nt(g_t_ref[...], active_ref[...])

    def emit_fc1(place):
        for group in range(chunk // 16):
            at = step * (chunk // 32 * rows) + (group // 2) * rows
            to = pl.ds(pl.multiple_of(at, rows), 16)
            ref = mine_ref if group % 2 == place else other_ref
            ref[to, :] = fc1_low[group * 16 : (group + 1) * 16]

    by_place(core, emit_fc1)

    def emit_fc2(place):
        @pl.loop(0, channels // 8)
        def _(pair):
            at = pl.ds(pl.multiple_of(pair * 8, 8), 8)
            taken = [fc2_sum_ref[s, at, :] for s in range(4)]
            to = pl.ds(pl.multiple_of(pair * rows + 16, 16), 16)
            for half in range(2):
                block = jnp.concatenate([t[4 * half : 4 * half + 4] for t in taken], axis=0)
                ref = mine_ref if half == place else other_ref
                ref[to, :] = block.astype(BF16)

    @pl.when(step == pl.num_programs(0) - 1)
    def _():
        by_place(core, emit_fc2)


def feed_forward(core, g_own, g_side, g_below, g_corner, act2, gain2, fc1_weight, fc2_weight):
    channels, tokens = act2.shape
    hidden = fc1_weight.shape[0]
    chunk = hidden // 4
    whole = lambda shape: pl.BlockSpec(shape, lambda s: (0,) * len(shape))
    return pl.pallas_call(
        feed_forward_kernel,
        grid=(hidden // chunk,),
        in_specs=[
            pl.BlockSpec(memory_space=pltpu.SMEM),
            whole(g_own.shape),
            whole(g_side.shape),
            whole(g_below.shape),
            whole(g_corner.shape),
            whole((channels, tokens)),
            whole((1, channels)),
            pl.BlockSpec((chunk, channels), lambda s: (s, 0)),
            pl.BlockSpec((channels, chunk), lambda s: (0, s)),
        ],
        out_specs=[
            whole((hidden, channels)),
            whole((hidden, channels)),
            whole((channels, tokens)),
            whole((1, channels)),
            whole((channels, tokens)),
        ],
        out_shape=[
            jax.ShapeDtypeStruct((hidden, channels), BF16),
            jax.ShapeDtypeStruct((hidden, channels), BF16),
            jax.ShapeDtypeStruct((channels, tokens), F32),
            jax.ShapeDtypeStruct((1, channels), F32),
            jax.ShapeDtypeStruct((channels, tokens), BF16),
        ],
        scratch_shapes=[
            pltpu.VMEM((hidden // chunk, channels, chunk), F32),
            pltpu.VMEM((chunk, tokens), BF16),
            pltpu.VMEM((chunk, tokens), BF16),
        ],
        compiler_params=pltpu.CompilerParams(vmem_limit_bytes=64 * 2**20),
        name="feed_forward",
    )(core, g_own, g_side, g_below, g_corner, act2, gain2[None, :], fc1_weight, fc2_weight)


def backward_kernel(
    totals, place_ref, g_t_ref, grad_act2_ref, normed2_ref, inv2_ref, heads_ref, mixed_ref, lse_ref, act1_ref,
    normed1_ref, inv1_ref, gain1_ref, gain2_ref, gain2_sum_ref, qkv_ref, proj_ref,
    dx_left_ref, dx_right_ref, mine_ref, other_ref,
    mask_ref, grad_mixed_ref, grad_heads_ref, qkv_sum_ref, proj_sum_ref, qkv_t_ref, proj_t_ref, gains_ref,
):
    step = pl.program_id(0)
    channels = grad_act2_ref.shape[0]
    head_dim = channels // HEADS

    @pl.when(step == 0)
    def _():
        qkv_sum_ref[...] = jnp.zeros_like(qkv_sum_ref)
        proj_sum_ref[...] = jnp.zeros_like(proj_sum_ref)
        qkv_t_ref[...] = qkv_ref[...].T
        proj_t_ref[...] = proj_ref[...].T

    mask_ref[...] = same_region(place_ref, step, totals)
    resid = g_t_ref[...].astype(F32) + norm_back(
        grad_act2_ref[...] * column(gain2_ref[...], 2), normed2_ref[...], inv2_ref[...]
    )
    low = resid.astype(BF16)
    grad_mixed_ref[...] = nn(proj_t_ref[...], low).astype(BF16)
    proj_sum_ref[...] += nt(low, mixed_ref[...])

    def spans(head):
        at = head * head_dim
        return [pl.ds(group * channels + at, head_dim) for group in range(3)]

    def score(head):
        q, k, v = spans(head)
        return (
            tn(heads_ref[k, :], heads_ref[q, :]),
            tn(heads_ref[v, :], grad_mixed_ref[q, :]),
        )

    def soften(head, pair):
        scores, grad_probs = pair
        scores = jnp.where(mask_ref[...] > 0.5, scores, MASKED)
        probs = jnp.exp(scores - lse_ref[0, pl.ds(head, 1), :])
        cross = jnp.sum(probs * grad_probs, axis=0, keepdims=True)
        return probs.astype(BF16), (probs * (grad_probs - cross)).astype(BF16)

    def mix(head, pair):
        probs_low, scores_low = pair
        q, k, v = spans(head)
        grad_heads_ref[v, :] = nt(grad_mixed_ref[q, :], probs_low).astype(BF16)
        grad_heads_ref[q, :] = (nn(heads_ref[k, :], scores_low) * (head_dim ** (-0.5))).astype(BF16)
        grad_heads_ref[k, :] = nt(heads_ref[q, :], scores_low).astype(BF16)

    staged(HEADS, 1, score, soften, mix)
    grad_act1 = nn(qkv_t_ref[...], grad_heads_ref[...]).astype(BF16).astype(F32)
    qkv_sum_ref[...] += nt(grad_heads_ref[...], act1_ref[...])
    dx = resid + norm_back(grad_act1 * column(gain1_ref[...], 2), normed1_ref[...], inv1_ref[...])
    dx = dx.T.astype(BF16)
    half = dx.shape[0] // 2
    dx_left_ref[...] = dx[:half]
    dx_right_ref[...] = dx[half:]

    def emit(place):
        @pl.loop(0, channels // 16)
        def _(four):
            at = pl.ds(pl.multiple_of(four * 16, 16), 16)
            qkv = qkv_sum_ref[pl.ds(pl.multiple_of(four * 48, 16), 48), :]
            proj = proj_sum_ref[at, :]
            gain = gains_ref[at, :]
            zeros = jnp.zeros((4, 128), F32)
            for half in range(2):
                ref = mine_ref if half == place else other_ref
                tops, lows, sides = [], [], []
                for pair in range(2):
                    device = 2 * pair + half
                    rows = qkv[12 * device : 12 * device + 12]
                    tops.append(rows[:8])
                    lows += [rows[8:], proj[4 * device : 4 * device + 4]]
                    sides += [zeros, gain[4 * device : 4 * device + 4]]
                for index, blocks in enumerate((tops, lows, sides)):
                    block = jnp.concatenate(blocks, axis=0).astype(BF16)
                    ref[at, pl.ds(index * channels, block.shape[1])] = block

    @pl.when(step == pl.num_programs(0) - 1)
    def _():
        gain1_sum = jnp.sum(
            qkv_sum_ref[...] * qkv_ref[...].astype(F32), axis=0, keepdims=True
        ) / gain1_ref[...]
        lines = lax.broadcasted_iota(jnp.int32, (128, channels), 0)
        gains_ref[...] = jnp.where(
            lines == 0, gain1_sum, jnp.where(lines == 1, gain2_sum_ref[...], 0.0)
        ).T
        by_place(place_ref[0], emit)


def backward(
    totals, place, g_t, grad_act2, normed2, inv2, heads, mixed, lse, act1, normed1, inv1,
    gain1, gain2, gain2_sum, qkv_weight, proj_weight,
):
    channels, tokens = grad_act2.shape
    window = WIN * WIN
    windows = tokens // window
    whole = lambda shape: pl.BlockSpec(shape, lambda w: (0,) * len(shape))
    feature = lambda rows: pl.BlockSpec((rows, window), lambda w: (0, w))
    packed = (channels, 2 * channels + 128)
    return pl.pallas_call(
        functools.partial(backward_kernel, totals),
        grid=(windows,),
        in_specs=[
            pl.BlockSpec(memory_space=pltpu.SMEM),
            feature(channels),
            feature(channels),
            feature(channels),
            feature(1),
            feature(3 * channels),
            feature(channels),
            pl.BlockSpec((1, HEADS, window), lambda w: (w, 0, 0)),
            feature(channels),
            feature(channels),
            feature(1),
            whole((1, channels)),
            whole((1, channels)),
            whole((1, channels)),
            whole(qkv_weight.shape),
            whole(proj_weight.shape),
        ],
        out_specs=[
            pl.BlockSpec((window // 2, channels), lambda w: (w, 0)),
            pl.BlockSpec((window // 2, channels), lambda w: (w, 0)),
            whole(packed),
            whole(packed),
        ],
        out_shape=[
            jax.ShapeDtypeStruct((tokens // 2, channels), BF16),
            jax.ShapeDtypeStruct((tokens // 2, channels), BF16),
            jax.ShapeDtypeStruct(packed, BF16),
            jax.ShapeDtypeStruct(packed, BF16),
        ],
        scratch_shapes=[
            pltpu.VMEM((window, window), F32),
            pltpu.VMEM((channels, window), BF16),
            pltpu.VMEM((3 * channels, window), BF16),
            pltpu.VMEM((3 * channels, channels), F32),
            pltpu.VMEM((channels, channels), F32),
            pltpu.VMEM((channels, 3 * channels), BF16),
            pltpu.VMEM((channels, channels), BF16),
            pltpu.VMEM((channels, 128), F32),
        ],
        compiler_params=pltpu.CompilerParams(vmem_limit_bytes=64 * 2**20),
        cost_estimate=pl.CostEstimate(
            flops=30 * tokens * channels * window,
            bytes_accessed=20 * tokens * channels,
            transcendentals=HEADS * tokens * window,
        ),
        name="attention_backward",
    )(
        place, g_t, grad_act2, normed2, inv2, heads, mixed, lse, act1, normed1, inv1,
        gain1[None, :], gain2[None, :], gain2_sum, qkv_weight, proj_weight,
    )


def unpack_kernel(factor, pieces_ref, qkv_out_ref, proj_out_ref, gain1_out_ref, gain2_out_ref, sum_ref):
    step = pl.program_id(0)

    @pl.when(step == 0)
    def _():
        sum_ref[...] = jnp.zeros_like(sum_ref)

    total = sum_ref[...]
    for piece in range(pieces_ref.shape[0]):
        total += pieces_ref[piece].astype(F32)
    sum_ref[...] = total

    @pl.when(step == pl.num_programs(0) - 1)
    def _():
        rows, channels = qkv_out_ref.shape
        scaled = sum_ref[...] * factor
        height = scaled.shape[0]
        rest = rows - height
        qkv_out_ref[pl.ds(0, height), :] = scaled[:, :channels]
        qkv_out_ref[pl.ds(height, rest), :] = scaled[:rest, channels : 2 * channels]
        proj_out_ref[...] = scaled[rest:, channels : 2 * channels]
        gains = jnp.concatenate([scaled[:, 2 * channels :]] * 16, axis=0).T
        gain1_out_ref[...] = gains[0:1, rest:height]
        gain2_out_ref[...] = gains[1:2, rest:height]


def unpack(pieces, rows, factor):
    chips, both, columns = pieces.shape
    channels = (columns - 128) // 2
    rest = 2 * both - rows
    shapes = [(rows, channels), (rest, channels), (1, rest), (1, rest)]
    return pl.pallas_call(
        functools.partial(unpack_kernel, factor),
        grid=(2,),
        in_specs=[pl.BlockSpec((chips // 2, both, columns), lambda s: (s, 0, 0))],
        out_specs=[pl.BlockSpec(shape, lambda s: (0, 0)) for shape in shapes],
        out_shape=[jax.ShapeDtypeStruct(shape, F32) for shape in shapes],
        scratch_shapes=[pltpu.VMEM((both, columns), F32)],
        compiler_params=pltpu.CompilerParams(vmem_limit_bytes=64 * 2**20),
        name="unpack",
    )(pieces)


def unpack_ffn_kernel(factor, pieces_ref, fc1_out_ref, fc2_out_ref, sum_ref):
    step = pl.program_id(0)

    @pl.when(step == 0)
    def _():
        sum_ref[...] = jnp.zeros_like(sum_ref)

    total = sum_ref[...]
    for piece in range(pieces_ref.shape[0]):
        total += pieces_ref[piece].astype(F32)
    sum_ref[...] = total

    @pl.when(step == pl.num_programs(0) - 1)
    def _():
        rows, channels = fc1_out_ref.shape
        scaled = sum_ref[...] * factor
        fc1_out_ref[...] = scaled[:rows]
        for part in range(fc2_out_ref.shape[1] // channels):
            at = rows + 4 * part
            fc2_out_ref[:, pl.ds(part * channels, channels)] = scaled[at : at + 4]


def unpack_ffn(pieces, fc1_rows, factor):
    chips, rows, channels = pieces.shape
    fc2_rows = (rows - fc1_rows) // 4
    shapes = [(fc1_rows, channels), (fc2_rows, 4 * channels)]
    return pl.pallas_call(
        functools.partial(unpack_ffn_kernel, factor),
        grid=(4,),
        in_specs=[pl.BlockSpec((chips // 4, rows, channels), lambda s: (s, 0, 0))],
        out_specs=[pl.BlockSpec(shape, lambda s: (0, 0)) for shape in shapes],
        out_shape=[jax.ShapeDtypeStruct(shape, F32) for shape in shapes],
        scratch_shapes=[pltpu.VMEM((rows, channels), F32)],
        compiler_params=pltpu.CompilerParams(vmem_limit_bytes=64 * 2**20),
        cost_estimate=pl.CostEstimate(
            flops=2**30, bytes_accessed=2 * chips * rows * channels, transcendentals=0
        ),
        name="unpack_ffn",
    )(pieces)


def diagonal(block, distance):
    rows = lax.axis_size("zl") * lax.axis_size("y")
    cols = lax.axis_size("zh") * lax.axis_size("x") * lax.axis_size("core")
    route = [
        ((r - distance) % rows * cols + (c - distance) % cols, r * cols + c) for r in range(rows) for c in range(cols)
    ]
    return lax.ppermute(block, ALL, route)


def roll_out(left, right):
    before = ring(right, COLS, 1)[:-SHIFT]
    above = ring(left[-SHIFT:], ROWS, 1)
    corner = diagonal(right[-SHIFT:], 1)
    top = jnp.concatenate([corner, above], axis=1)
    rest = jnp.concatenate([before, left[:-SHIFT]], axis=1)
    return jnp.concatenate([top, rest], axis=0)


def core_sum(mine, other):
    got = lax.ppermute(other, "core", [(0, 1), (1, 0)])
    return (mine.astype(F32) + got.astype(F32)).astype(BF16)


def chips_exchange(part):
    chips = 1
    for axis in CHIPS:
        chips *= lax.axis_size(axis)
    return lax.all_to_all(part.reshape(chips, -1, part.shape[1]), CHIPS, 0, 0, tiled=True)


def shards(tokens, cotangent, gain1, qkv_weight, proj_weight, gain2, fc1_weight, fc2_weight):
    tile_rows, tile_cols, channels = tokens.shape
    devices = 1
    for axis in ALL:
        devices *= lax.axis_size(axis)
    rows_total = tile_rows * lax.axis_size("zl") * lax.axis_size("y")
    cols_total = tile_cols * (devices * tile_rows // rows_total)
    totals = (rows_total, cols_total)
    place = jnp.stack(
        [
            lax.axis_index("core"),
            lax.axis_index(ROWS) * tile_rows,
            lax.axis_index(COLS) * tile_cols,
        ]
    ).astype(jnp.int32)
    flat = lambda block: block.reshape(-1, channels)
    x_out, tokens, cotangent = lax.optimization_barrier((tokens[SHIFT:, :SHIFT], tokens, cotangent))
    x_side = flat(ring(x_out, COLS, -1))
    first = jnp.stack([tokens[:SHIFT], cotangent[:SHIFT]])
    below = ring(first[:, :, SHIFT:], ROWS, -1)
    corner = diagonal(first[:, :, :SHIFT], -1)
    g_side = flat(ring(cotangent[SHIFT:, :SHIFT], COLS, -1))
    x_own = flat(tokens[SHIFT:, SHIFT:])
    g_own = flat(cotangent[SHIFT:, SHIFT:])
    heads, mixed, act1, normed1, inv1, lse, normed2, inv2, act2 = forward(
        totals, place, x_own, x_side, flat(below[0]), flat(corner[0]), qkv_weight, proj_weight,
        gain1, gain2,
    )
    ffn_mine, ffn_other, grad_act2, gain2_sum, g_t = feed_forward(
        place, g_own, g_side, flat(below[1]), flat(corner[1]), act2, gain2, fc1_weight, fc2_weight
    )
    ffn_chip = core_sum(ffn_mine, ffn_other)
    grad_act2, ffn_chip = lax.optimization_barrier((grad_act2, ffn_chip))
    ffn_pieces = chips_exchange(ffn_chip)
    dx_left, dx_right, att_mine, att_other = backward(
        totals, place, g_t, grad_act2, normed2, inv2, heads, mixed, lse, act1, normed1, inv1,
        gain1, gain2, gain2_sum, qkv_weight, proj_weight,
    )
    halves = (tile_rows, SHIFT, channels)
    grad_tokens = roll_out(dx_left.reshape(halves), dx_right.reshape(halves))
    att_chip = core_sum(att_mine, att_other)
    att_chip, grad_tokens = lax.optimization_barrier((att_chip, grad_tokens))
    norm_factor = (rows_total * cols_total) ** (-0.5)
    qkv_rows = qkv_weight.shape[0] // devices
    qkv_out, proj_out, gain1_out, gain2_out = unpack(
        chips_exchange(att_chip), qkv_rows, norm_factor
    )
    fc1_out, fc2_out = unpack_ffn(ffn_pieces, fc1_weight.shape[0] // devices, norm_factor)
    return (
        grad_tokens,
        qkv_out,
        proj_out,
        fc1_out,
        fc2_out,
        gain1_out.reshape(-1),
        gain2_out.reshape(-1),
    )


def solution(mesh):
    fine = Mesh(mesh.devices.reshape(2, 4, 2, 4, 2), ALL)
    return jax.shard_map(
        shards,
        mesh=fine,
        in_specs=(P(ROWS, COLS, None), P(ROWS, COLS, None), P(), P(), P(), P(), P(), P()),
        out_specs=(
            P(ROWS, COLS, None),
            P(ALL, None),
            P(ALL, None),
            P(ALL, None),
            P(ALL, None),
            P(ALL),
            P(ALL),
        ),
        check_vma=False,
    )
```

```python
import functools

import jax
import jax.numpy as jnp
from jax import lax
from jax.experimental import pallas as pl
from jax.experimental.pallas import tpu as pltpu
from jax.sharding import Mesh, PartitionSpec as P

HEADS = 16
WIN = 16
SHIFT = 8

EPS = 1e-05
MASKED = -1000000000.0
ROOT_HALF = 0.7071067811865476
INV_ROOT_TAU = 0.3989422804014327

F32 = jnp.float32
BF16 = jnp.bfloat16
ROWS = ("zl", "y")
COLS = ("zh", "x", "core")
CHIPS = ("zl", "y", "zh", "x")
ALL = ROWS + COLS


def nn(a, b):
    return lax.dot_general(a, b, (((1,), (0,)), ((), ())), preferred_element_type=F32)


def nt(a, b):
    return lax.dot_general(a, b, (((1,), (1,)), ((), ())), preferred_element_type=F32)


def tn(a, b):
    return lax.dot_general(a, b, (((0,), (0,)), ((), ())), preferred_element_type=F32)


def ring(block, axes, distance):
    size = 1
    for axis in axes:
        size *= lax.axis_size(axis)
    route = [((i - distance) % size, i) for i in range(size)]
    return lax.ppermute(block, axes, route)


def norm_stats(values):
    average = jnp.mean(values, axis=0, keepdims=True)
    centred = values - average
    variance = jnp.mean(centred * centred, axis=0, keepdims=True)
    inverse = lax.rsqrt(variance + EPS)
    return centred * inverse, inverse


def norm_back(grad_normed, normed, inverse):
    mean_grad = jnp.mean(grad_normed, axis=0, keepdims=True)
    mean_cross = jnp.mean(grad_normed * normed, axis=0, keepdims=True)
    return (grad_normed - mean_grad - normed * mean_cross) * inverse


def staged(count, lead, first, second, third):
    opened, closed = {}, {}
    for turn in range(count + lead + 1):
        if turn < count:
            opened[turn] = first(turn)
        if 0 <= turn - lead < count:
            closed[turn - lead] = second(turn - lead, opened.pop(turn - lead))
        if 0 <= turn - lead - 1 < count:
            third(turn - lead - 1, closed.pop(turn - lead - 1))


def by_place(core, emit):
    for place in range(2):

        @pl.when(core == place)
        def _():
            emit(place)


def region(coords, total):
    return jnp.where(coords < total - WIN, 0, jnp.where(coords < total - SHIFT, 1, 2)).astype(
        jnp.int32
    )


def column(row, copies):
    block = jnp.broadcast_to(row, (128, row.shape[1])).T
    return jnp.concatenate([block] * copies, axis=1)


def same_region(place_ref, window, totals):
    tokens = WIN * WIN

    def labels(shape, dim):
        token = lax.broadcasted_iota(jnp.int32, shape, dim)
        down = place_ref[1] + window * WIN + token % (tokens // 2) // SHIFT
        along = place_ref[2] + token // (tokens // 2) * SHIFT + token % SHIFT
        return 3 * region(down, totals[0]) + region(along, totals[1])

    return (labels((tokens, tokens), 0) == labels((tokens, tokens), 1)).astype(F32)


def forward_kernel(
    totals, place_ref, x_own_ref, x_own_next_ref, x_side_ref, x_side_next_ref, x_below_ref, x_corner_ref, qkv_ref, proj_ref, gain1_ref, gain2_ref,
    heads_ref, mixed_ref, act1_ref, normed1_ref, inv1_ref, lse_ref, normed2_ref, inv2_ref, act2_ref,
    mask_ref,
):
    channels = x_own_ref.shape[1]
    head_dim = channels // HEADS
    last = pl.program_id(0) == pl.num_programs(0) - 1
    pieces = [
        x_own_ref[...].astype(F32),
        jnp.where(last, x_below_ref[...].astype(F32), x_own_next_ref[...].astype(F32)),
        x_side_ref[...].astype(F32),
        jnp.where(last, x_corner_ref[...].astype(F32), x_side_next_ref[...].astype(F32)),
    ]
    x = jnp.concatenate(pieces, axis=0).T
    normed1, inverse1 = norm_stats(x)
    act1 = (normed1 * column(gain1_ref[...], 2)).astype(BF16)
    act1_ref[...] = act1
    normed1_ref[...] = normed1
    inv1_ref[...] = inverse1
    queries = nn(qkv_ref[pl.ds(0, channels), :], act1) * (head_dim ** (-0.5))
    heads_ref[pl.ds(0, channels), :] = queries.astype(BF16)
    heads_ref[pl.ds(channels, 2 * channels), :] = nn(
        qkv_ref[pl.ds(channels, 2 * channels), :], act1
    ).astype(BF16)
    mask_ref[...] = same_region(place_ref, pl.program_id(0), totals)

    def score(head):
        at = head * head_dim
        return tn(heads_ref[pl.ds(channels + at, head_dim), :], heads_ref[pl.ds(at, head_dim), :])

    def soften(head, scores):
        scores = jnp.where(mask_ref[...] > 0.5, scores, MASKED)
        highest = jnp.max(scores, axis=0, keepdims=True)
        raised = jnp.exp(scores - highest)
        total = jnp.sum(raised, axis=0, keepdims=True)
        lse_ref[0, pl.ds(head, 1), :] = highest + jnp.log(total)
        return (raised * (1.0 / total)).astype(BF16)

    def mix(head, probs_low):
        at = head * head_dim
        value = heads_ref[pl.ds(2 * channels + at, head_dim), :]
        mixed_ref[pl.ds(at, head_dim), :] = nn(value, probs_low).astype(BF16)

    staged(HEADS, 2, score, soften, mix)
    attn = nn(proj_ref[...], mixed_ref[...]).astype(BF16)
    normed2, inverse2 = norm_stats(x + attn.astype(F32))
    normed2_ref[...] = normed2
    inv2_ref[...] = inverse2
    act2_ref[...] = (normed2 * column(gain2_ref[...], 2)).astype(BF16)


def forward(totals, place, x_own, x_side, x_below, x_corner, qkv_weight, proj_weight, gain1, gain2):
    quarter, channels = x_below.shape
    tokens = 2 * (x_own.shape[0] + quarter)
    window = WIN * WIN
    windows = tokens // window
    whole = lambda shape: pl.BlockSpec(shape, lambda w: (0,) * len(shape))
    feature = lambda rows: pl.BlockSpec((rows, window), lambda w: (0, w))
    here = pl.BlockSpec((quarter, channels), lambda w: (2 * w, 0))
    following = pl.BlockSpec(
        (quarter, channels), lambda w: (jnp.minimum(2 * w + 1, 2 * windows - 2), 0)
    )
    return pl.pallas_call(
        functools.partial(forward_kernel, totals),
        grid=(windows,),
        in_specs=[
            pl.BlockSpec(memory_space=pltpu.SMEM),
            here,
            following,
            here,
            following,
            whole(x_below.shape),
            whole(x_corner.shape),
            whole(qkv_weight.shape),
            whole(proj_weight.shape),
            whole((1, channels)),
            whole((1, channels)),
        ],
        out_specs=[
            feature(3 * channels),
            feature(channels),
            feature(channels),
            feature(channels),
            feature(1),
            pl.BlockSpec((1, HEADS, window), lambda w: (w, 0, 0)),
            feature(channels),
            feature(1),
            feature(channels),
        ],
        out_shape=[
            jax.ShapeDtypeStruct((3 * channels, tokens), BF16),
            jax.ShapeDtypeStruct((channels, tokens), BF16),
            jax.ShapeDtypeStruct((channels, tokens), BF16),
            jax.ShapeDtypeStruct((channels, tokens), F32),
            jax.ShapeDtypeStruct((1, tokens), F32),
            jax.ShapeDtypeStruct((windows, HEADS, window), F32),
            jax.ShapeDtypeStruct((channels, tokens), F32),
            jax.ShapeDtypeStruct((1, tokens), F32),
            jax.ShapeDtypeStruct((channels, tokens), BF16),
        ],
        scratch_shapes=[pltpu.VMEM((window, window), F32)],
        compiler_params=pltpu.CompilerParams(vmem_limit_bytes=64 * 2**20),
        name="attention_forward",
    )(
        place, x_own, x_own, x_side, x_side, x_below, x_corner, qkv_weight, proj_weight,
        gain1[None, :], gain2[None, :],
    )


def feed_forward_kernel(
    core_ref, g_own_ref, g_side_ref, g_below_ref, g_corner_ref, act2_ref, gain2_ref, fc1_ref, fc2_ref,
    mine_ref, other_ref, grad_act2_ref, gain_ref, g_t_ref,
    fc2_sum_ref, active_ref, grad_hidden_ref,
):
    step = pl.program_id(0)
    core = core_ref[0]
    channels, tokens = act2_ref.shape
    chunk = fc1_ref.shape[0]
    rows = 32
    piece = 256

    @pl.when(step == 0)
    def _():
        half = WIN * SHIFT
        halves = [(g_own_ref, g_below_ref), (g_side_ref, g_corner_ref)]
        for window in range(tokens // (2 * half)):
            at = window * half
            pieces = []
            for ref, last_ref in halves:
                if at + half <= ref.shape[0]:
                    pieces.append(ref[pl.ds(at, half), :])
                else:
                    pieces += [ref[pl.ds(at, half // 2), :], last_ref[...]]
            joined = jnp.concatenate([piece.astype(F32) for piece in pieces], axis=0)
            g_t_ref[:, pl.ds(2 * at, 2 * half)] = joined.T.astype(BF16)
        grad_act2_ref[...] = jnp.zeros_like(grad_act2_ref)
        gain_ref[...] = jnp.zeros_like(gain_ref)

    def project(index):
        span = pl.ds(index * piece, piece)
        return nn(fc1_ref[...], act2_ref[:, span]), tn(fc2_ref[...], g_t_ref[:, span])

    def bend(index, pair):
        span = pl.ds(index * piece, piece)
        hidden, grad_active = pair
        grad_active = grad_active.astype(BF16).astype(F32)
        bell = 0.5 * (1.0 + lax.erf(hidden * ROOT_HALF))
        slope = bell + hidden * INV_ROOT_TAU * jnp.exp(-0.5 * hidden * hidden)
        grad_hidden = (grad_active * slope).astype(BF16)
        active_ref[:, span] = (hidden * bell).astype(BF16)
        grad_hidden_ref[:, span] = grad_hidden
        return grad_hidden

    def back(index, grad_hidden):
        grad_act2_ref[:, pl.ds(index * piece, piece)] += tn(fc1_ref[...], grad_hidden)

    staged(tokens // piece, 1, project, bend, back)
    fc1_part = nt(grad_hidden_ref[...], act2_ref[...])
    gain_ref[...] += jnp.sum(
        fc1_part * fc1_ref[...].astype(F32), axis=0, keepdims=True
    ) / gain2_ref[...]
    fc1_low = fc1_part.astype(BF16)
    fc2_sum_ref[step] = nt(g_t_ref[...], active_ref[...])

    def emit_fc1(place):
        for group in range(chunk // 16):
            at = step * (chunk // 32 * rows) + (group // 2) * rows
            to = pl.ds(pl.multiple_of(at, rows), 16)
            ref = mine_ref if group % 2 == place else other_ref
            ref[to, :] = fc1_low[group * 16 : (group + 1) * 16]

    by_place(core, emit_fc1)

    def emit_fc2(place):
        @pl.loop(0, channels // 8)
        def _(pair):
            at = pl.ds(pl.multiple_of(pair * 8, 8), 8)
            taken = [fc2_sum_ref[s, at, :] for s in range(4)]
            to = pl.ds(pl.multiple_of(pair * rows + 16, 16), 16)
            for half in range(2):
                block = jnp.concatenate([t[4 * half : 4 * half + 4] for t in taken], axis=0)
                ref = mine_ref if half == place else other_ref
                ref[to, :] = block.astype(BF16)

    @pl.when(step == pl.num_programs(0) - 1)
    def _():
        by_place(core, emit_fc2)


def feed_forward(core, g_own, g_side, g_below, g_corner, act2, gain2, fc1_weight, fc2_weight):
    channels, tokens = act2.shape
    hidden = fc1_weight.shape[0]
    chunk = hidden // 4
    whole = lambda shape: pl.BlockSpec(shape, lambda s: (0,) * len(shape))
    return pl.pallas_call(
        feed_forward_kernel,
        grid=(hidden // chunk,),
        in_specs=[
            pl.BlockSpec(memory_space=pltpu.SMEM),
            whole(g_own.shape),
            whole(g_side.shape),
            whole(g_below.shape),
            whole(g_corner.shape),
            whole((channels, tokens)),
            whole((1, channels)),
            pl.BlockSpec((chunk, channels), lambda s: (s, 0)),
            pl.BlockSpec((channels, chunk), lambda s: (0, s)),
        ],
        out_specs=[
            whole((hidden, channels)),
            whole((hidden, channels)),
            whole((channels, tokens)),
            whole((1, channels)),
            whole((channels, tokens)),
        ],
        out_shape=[
            jax.ShapeDtypeStruct((hidden, channels), BF16),
            jax.ShapeDtypeStruct((hidden, channels), BF16),
            jax.ShapeDtypeStruct((channels, tokens), F32),
            jax.ShapeDtypeStruct((1, channels), F32),
            jax.ShapeDtypeStruct((channels, tokens), BF16),
        ],
        scratch_shapes=[
            pltpu.VMEM((hidden // chunk, channels, chunk), F32),
            pltpu.VMEM((chunk, tokens), BF16),
            pltpu.VMEM((chunk, tokens), BF16),
        ],
        compiler_params=pltpu.CompilerParams(vmem_limit_bytes=64 * 2**20),
        name="feed_forward",
    )(core, g_own, g_side, g_below, g_corner, act2, gain2[None, :], fc1_weight, fc2_weight)


def backward_kernel(
    totals, place_ref, g_t_ref, grad_act2_ref, normed2_ref, inv2_ref, heads_ref, mixed_ref, lse_ref, act1_ref,
    normed1_ref, inv1_ref, gain1_ref, gain2_ref, gain2_sum_ref, qkv_ref, proj_ref,
    dx_left_ref, dx_right_ref, mine_ref, other_ref,
    mask_ref, grad_mixed_ref, grad_heads_ref, qkv_sum_ref, proj_sum_ref, qkv_t_ref, proj_t_ref, gains_ref,
):
    step = pl.program_id(0)
    channels = grad_act2_ref.shape[0]
    head_dim = channels // HEADS

    @pl.when(step == 0)
    def _():
        qkv_sum_ref[...] = jnp.zeros_like(qkv_sum_ref)
        proj_sum_ref[...] = jnp.zeros_like(proj_sum_ref)
        qkv_t_ref[...] = qkv_ref[...].T
        proj_t_ref[...] = proj_ref[...].T

    mask_ref[...] = same_region(place_ref, step, totals)
    resid = g_t_ref[...].astype(F32) + norm_back(
        grad_act2_ref[...] * column(gain2_ref[...], 2), normed2_ref[...], inv2_ref[...]
    )
    low = resid.astype(BF16)
    grad_mixed_ref[...] = nn(proj_t_ref[...], low).astype(BF16)
    proj_sum_ref[...] += nt(low, mixed_ref[...])

    def spans(head):
        at = head * head_dim
        return [pl.ds(group * channels + at, head_dim) for group in range(3)]

    def score(head):
        q, k, v = spans(head)
        return (
            tn(heads_ref[k, :], heads_ref[q, :]),
            tn(heads_ref[v, :], grad_mixed_ref[q, :]),
        )

    def soften(head, pair):
        scores, grad_probs = pair
        scores = jnp.where(mask_ref[...] > 0.5, scores, MASKED)
        probs = jnp.exp(scores - lse_ref[0, pl.ds(head, 1), :])
        own = spans(head)[0]
        cross = jnp.sum(
            grad_mixed_ref[own, :].astype(F32) * mixed_ref[own, :].astype(F32), axis=0, keepdims=True
        )
        return probs.astype(BF16), (probs * (grad_probs - cross)).astype(BF16)

    def mix(head, pair):
        probs_low, scores_low = pair
        q, k, v = spans(head)
        grad_heads_ref[v, :] = nt(grad_mixed_ref[q, :], probs_low).astype(BF16)
        grad_heads_ref[q, :] = (nn(heads_ref[k, :], scores_low) * (head_dim ** (-0.5))).astype(BF16)
        grad_heads_ref[k, :] = nt(heads_ref[q, :], scores_low).astype(BF16)

    staged(HEADS, 1, score, soften, mix)
    grad_act1 = nn(qkv_t_ref[...], grad_heads_ref[...]).astype(BF16).astype(F32)
    qkv_sum_ref[...] += nt(grad_heads_ref[...], act1_ref[...])
    dx = resid + norm_back(grad_act1 * column(gain1_ref[...], 2), normed1_ref[...], inv1_ref[...])
    dx = dx.T.astype(BF16)
    half = dx.shape[0] // 2
    dx_left_ref[...] = dx[:half]
    dx_right_ref[...] = dx[half:]

    def emit(place):
        @pl.loop(0, channels // 16)
        def _(four):
            at = pl.ds(pl.multiple_of(four * 16, 16), 16)
            qkv = qkv_sum_ref[pl.ds(pl.multiple_of(four * 48, 16), 48), :]
            proj = proj_sum_ref[at, :]
            gain = gains_ref[at, :]
            zeros = jnp.zeros((4, 128), F32)
            for half in range(2):
                ref = mine_ref if half == place else other_ref
                tops, lows, sides = [], [], []
                for pair in range(2):
                    device = 2 * pair + half
                    rows = qkv[12 * device : 12 * device + 12]
                    tops.append(rows[:8])
                    lows += [rows[8:], proj[4 * device : 4 * device + 4]]
                    sides += [zeros, gain[4 * device : 4 * device + 4]]
                for index, blocks in enumerate((tops, lows, sides)):
                    block = jnp.concatenate(blocks, axis=0).astype(BF16)
                    ref[at, pl.ds(index * channels, block.shape[1])] = block

    @pl.when(step == pl.num_programs(0) - 1)
    def _():
        gain1_sum = jnp.sum(
            qkv_sum_ref[...] * qkv_ref[...].astype(F32), axis=0, keepdims=True
        ) / gain1_ref[...]
        lines = lax.broadcasted_iota(jnp.int32, (128, channels), 0)
        gains_ref[...] = jnp.where(
            lines == 0, gain1_sum, jnp.where(lines == 1, gain2_sum_ref[...], 0.0)
        ).T
        by_place(place_ref[0], emit)


def backward(
    totals, place, g_t, grad_act2, normed2, inv2, heads, mixed, lse, act1, normed1, inv1,
    gain1, gain2, gain2_sum, qkv_weight, proj_weight,
):
    channels, tokens = grad_act2.shape
    window = WIN * WIN
    windows = tokens // window
    whole = lambda shape: pl.BlockSpec(shape, lambda w: (0,) * len(shape))
    feature = lambda rows: pl.BlockSpec((rows, window), lambda w: (0, w))
    packed = (channels, 2 * channels + 128)
    return pl.pallas_call(
        functools.partial(backward_kernel, totals),
        grid=(windows,),
        in_specs=[
            pl.BlockSpec(memory_space=pltpu.SMEM),
            feature(channels),
            feature(channels),
            feature(channels),
            feature(1),
            feature(3 * channels),
            feature(channels),
            pl.BlockSpec((1, HEADS, window), lambda w: (w, 0, 0)),
            feature(channels),
            feature(channels),
            feature(1),
            whole((1, channels)),
            whole((1, channels)),
            whole((1, channels)),
            whole(qkv_weight.shape),
            whole(proj_weight.shape),
        ],
        out_specs=[
            pl.BlockSpec((window // 2, channels), lambda w: (w, 0)),
            pl.BlockSpec((window // 2, channels), lambda w: (w, 0)),
            whole(packed),
            whole(packed),
        ],
        out_shape=[
            jax.ShapeDtypeStruct((tokens // 2, channels), BF16),
            jax.ShapeDtypeStruct((tokens // 2, channels), BF16),
            jax.ShapeDtypeStruct(packed, BF16),
            jax.ShapeDtypeStruct(packed, BF16),
        ],
        scratch_shapes=[
            pltpu.VMEM((window, window), F32),
            pltpu.VMEM((channels, window), BF16),
            pltpu.VMEM((3 * channels, window), BF16),
            pltpu.VMEM((3 * channels, channels), F32),
            pltpu.VMEM((channels, channels), F32),
            pltpu.VMEM((channels, 3 * channels), BF16),
            pltpu.VMEM((channels, channels), BF16),
            pltpu.VMEM((channels, 128), F32),
        ],
        compiler_params=pltpu.CompilerParams(vmem_limit_bytes=64 * 2**20),
        cost_estimate=pl.CostEstimate(
            flops=30 * tokens * channels * window,
            bytes_accessed=20 * tokens * channels,
            transcendentals=HEADS * tokens * window,
        ),
        name="attention_backward",
    )(
        place, g_t, grad_act2, normed2, inv2, heads, mixed, lse, act1, normed1, inv1,
        gain1[None, :], gain2[None, :], gain2_sum, qkv_weight, proj_weight,
    )


def unpack_kernel(factor, pieces_ref, qkv_out_ref, proj_out_ref, gain1_out_ref, gain2_out_ref, sum_ref):
    step = pl.program_id(0)

    @pl.when(step == 0)
    def _():
        sum_ref[...] = jnp.zeros_like(sum_ref)

    total = sum_ref[...]
    for piece in range(pieces_ref.shape[0]):
        total += pieces_ref[piece].astype(F32)
    sum_ref[...] = total

    @pl.when(step == pl.num_programs(0) - 1)
    def _():
        rows, channels = qkv_out_ref.shape
        scaled = sum_ref[...] * factor
        height = scaled.shape[0]
        rest = rows - height
        qkv_out_ref[pl.ds(0, height), :] = scaled[:, :channels]
        qkv_out_ref[pl.ds(height, rest), :] = scaled[:rest, channels : 2 * channels]
        proj_out_ref[...] = scaled[rest:, channels : 2 * channels]
        gains = jnp.concatenate([scaled[:, 2 * channels :]] * 16, axis=0).T
        gain1_out_ref[...] = gains[0:1, rest:height]
        gain2_out_ref[...] = gains[1:2, rest:height]


def unpack(pieces, rows, factor):
    chips, both, columns = pieces.shape
    channels = (columns - 128) // 2
    rest = 2 * both - rows
    shapes = [(rows, channels), (rest, channels), (1, rest), (1, rest)]
    return pl.pallas_call(
        functools.partial(unpack_kernel, factor),
        grid=(2,),
        in_specs=[pl.BlockSpec((chips // 2, both, columns), lambda s: (s, 0, 0))],
        out_specs=[pl.BlockSpec(shape, lambda s: (0, 0)) for shape in shapes],
        out_shape=[jax.ShapeDtypeStruct(shape, F32) for shape in shapes],
        scratch_shapes=[pltpu.VMEM((both, columns), F32)],
        compiler_params=pltpu.CompilerParams(vmem_limit_bytes=64 * 2**20),
        name="unpack",
    )(pieces)


def unpack_ffn_kernel(factor, pieces_ref, fc1_out_ref, fc2_out_ref, sum_ref):
    step = pl.program_id(0)

    @pl.when(step == 0)
    def _():
        sum_ref[...] = jnp.zeros_like(sum_ref)

    total = sum_ref[...]
    for piece in range(pieces_ref.shape[0]):
        total += pieces_ref[piece].astype(F32)
    sum_ref[...] = total

    @pl.when(step == pl.num_programs(0) - 1)
    def _():
        rows, channels = fc1_out_ref.shape
        scaled = sum_ref[...] * factor
        fc1_out_ref[...] = scaled[:rows]
        for part in range(fc2_out_ref.shape[1] // channels):
            at = rows + 4 * part
            fc2_out_ref[:, pl.ds(part * channels, channels)] = scaled[at : at + 4]


def unpack_ffn(pieces, fc1_rows, factor):
    chips, rows, channels = pieces.shape
    fc2_rows = (rows - fc1_rows) // 4
    shapes = [(fc1_rows, channels), (fc2_rows, 4 * channels)]
    return pl.pallas_call(
        functools.partial(unpack_ffn_kernel, factor),
        grid=(4,),
        in_specs=[pl.BlockSpec((chips // 4, rows, channels), lambda s: (s, 0, 0))],
        out_specs=[pl.BlockSpec(shape, lambda s: (0, 0)) for shape in shapes],
        out_shape=[jax.ShapeDtypeStruct(shape, F32) for shape in shapes],
        scratch_shapes=[pltpu.VMEM((rows, channels), F32)],
        compiler_params=pltpu.CompilerParams(vmem_limit_bytes=64 * 2**20),
        cost_estimate=pl.CostEstimate(
            flops=2**30, bytes_accessed=2 * chips * rows * channels, transcendentals=0
        ),
        name="unpack_ffn",
    )(pieces)


def diagonal(block, distance):
    rows = lax.axis_size("zl") * lax.axis_size("y")
    cols = lax.axis_size("zh") * lax.axis_size("x") * lax.axis_size("core")
    route = [
        ((r - distance) % rows * cols + (c - distance) % cols, r * cols + c) for r in range(rows) for c in range(cols)
    ]
    return lax.ppermute(block, ALL, route)


def roll_out(left, right):
    before = ring(right, COLS, 1)[:-SHIFT]
    above = ring(left[-SHIFT:], ROWS, 1)
    corner = diagonal(right[-SHIFT:], 1)
    top = jnp.concatenate([corner, above], axis=1)
    rest = jnp.concatenate([before, left[:-SHIFT]], axis=1)
    return jnp.concatenate([top, rest], axis=0)


def core_sum(mine, other):
    got = lax.ppermute(other, "core", [(0, 1), (1, 0)])
    return (mine.astype(F32) + got.astype(F32)).astype(BF16)


def chips_exchange(part):
    chips = 1
    for axis in CHIPS:
        chips *= lax.axis_size(axis)
    return lax.all_to_all(part.reshape(chips, -1, part.shape[1]), CHIPS, 0, 0, tiled=True)


def shards(tokens, cotangent, gain1, qkv_weight, proj_weight, gain2, fc1_weight, fc2_weight):
    tile_rows, tile_cols, channels = tokens.shape
    devices = 1
    for axis in ALL:
        devices *= lax.axis_size(axis)
    rows_total = tile_rows * lax.axis_size("zl") * lax.axis_size("y")
    cols_total = tile_cols * (devices * tile_rows // rows_total)
    totals = (rows_total, cols_total)
    place = jnp.stack(
        [
            lax.axis_index("core"),
            lax.axis_index(ROWS) * tile_rows,
            lax.axis_index(COLS) * tile_cols,
        ]
    ).astype(jnp.int32)
    flat = lambda block: block.reshape(-1, channels)
    x_out, tokens, cotangent = lax.optimization_barrier((tokens[SHIFT:, :SHIFT], tokens, cotangent))
    x_side = flat(ring(x_out, COLS, -1))
    first = jnp.stack([tokens[:SHIFT], cotangent[:SHIFT]])
    below = ring(first[:, :, SHIFT:], ROWS, -1)
    corner = diagonal(first[:, :, :SHIFT], -1)
    g_side = flat(ring(cotangent[SHIFT:, :SHIFT], COLS, -1))
    x_own = flat(tokens[SHIFT:, SHIFT:])
    g_own = flat(cotangent[SHIFT:, SHIFT:])
    heads, mixed, act1, normed1, inv1, lse, normed2, inv2, act2 = forward(
        totals, place, x_own, x_side, flat(below[0]), flat(corner[0]), qkv_weight, proj_weight,
        gain1, gain2,
    )
    ffn_mine, ffn_other, grad_act2, gain2_sum, g_t = feed_forward(
        place, g_own, g_side, flat(below[1]), flat(corner[1]), act2, gain2, fc1_weight, fc2_weight
    )
    ffn_chip = core_sum(ffn_mine, ffn_other)
    grad_act2, ffn_chip = lax.optimization_barrier((grad_act2, ffn_chip))
    ffn_pieces = chips_exchange(ffn_chip)
    dx_left, dx_right, att_mine, att_other = backward(
        totals, place, g_t, grad_act2, normed2, inv2, heads, mixed, lse, act1, normed1, inv1,
        gain1, gain2, gain2_sum, qkv_weight, proj_weight,
    )
    halves = (tile_rows, SHIFT, channels)
    grad_tokens = roll_out(dx_left.reshape(halves), dx_right.reshape(halves))
    att_chip = core_sum(att_mine, att_other)
    att_chip, grad_tokens = lax.optimization_barrier((att_chip, grad_tokens))
    norm_factor = (rows_total * cols_total) ** (-0.5)
    qkv_rows = qkv_weight.shape[0] // devices
    qkv_out, proj_out, gain1_out, gain2_out = unpack(
        chips_exchange(att_chip), qkv_rows, norm_factor
    )
    fc1_out, fc2_out = unpack_ffn(ffn_pieces, fc1_weight.shape[0] // devices, norm_factor)
    return (
        grad_tokens,
        qkv_out,
        proj_out,
        fc1_out,
        fc2_out,
        gain1_out.reshape(-1),
        gain2_out.reshape(-1),
    )


def solution(mesh):
    fine = Mesh(mesh.devices.reshape(2, 4, 2, 4, 2), ALL)
    return jax.shard_map(
        shards,
        mesh=fine,
        in_specs=(P(ROWS, COLS, None), P(ROWS, COLS, None), P(), P(), P(), P(), P(), P()),
        out_specs=(
            P(ROWS, COLS, None),
            P(ALL, None),
            P(ALL, None),
            P(ALL, None),
            P(ALL, None),
            P(ALL),
            P(ALL),
        ),
        check_vma=False,
    )
```

```python
import functools

import jax
import jax.numpy as jnp
from jax import lax
from jax.experimental import pallas as pl
from jax.experimental.pallas import tpu as pltpu
from jax.sharding import Mesh, PartitionSpec as P

HEADS = 16
WIN = 16
SHIFT = 8

EPS = 1e-05
MASKED = -1000000000.0
ROOT_HALF = 0.7071067811865476
INV_ROOT_TAU = 0.3989422804014327

F32 = jnp.float32
BF16 = jnp.bfloat16
ROWS = ("zl", "y")
COLS = ("zh", "x", "core")
CHIPS = ("zl", "y", "zh", "x")
ALL = ROWS + COLS


def nn(a, b):
    return lax.dot_general(a, b, (((1,), (0,)), ((), ())), preferred_element_type=F32)


def nt(a, b):
    return lax.dot_general(a, b, (((1,), (1,)), ((), ())), preferred_element_type=F32)


def tn(a, b):
    return lax.dot_general(a, b, (((0,), (0,)), ((), ())), preferred_element_type=F32)


def ring(block, axes, distance):
    size = 1
    for axis in axes:
        size *= lax.axis_size(axis)
    route = [((i - distance) % size, i) for i in range(size)]
    return lax.ppermute(block, axes, route)


def norm_stats(values):
    average = jnp.mean(values, axis=0, keepdims=True)
    centred = values - average
    variance = jnp.mean(centred * centred, axis=0, keepdims=True)
    inverse = lax.rsqrt(variance + EPS)
    return centred * inverse, inverse


def norm_back(grad_normed, normed, inverse):
    mean_grad = jnp.mean(grad_normed, axis=0, keepdims=True)
    mean_cross = jnp.mean(grad_normed * normed, axis=0, keepdims=True)
    return (grad_normed - mean_grad - normed * mean_cross) * inverse


def staged(count, lead, first, second, third):
    opened, closed = {}, {}
    for turn in range(count + lead + 1):
        if turn < count:
            opened[turn] = first(turn)
        if 0 <= turn - lead < count:
            closed[turn - lead] = second(turn - lead, opened.pop(turn - lead))
        if 0 <= turn - lead - 1 < count:
            third(turn - lead - 1, closed.pop(turn - lead - 1))


def by_place(core, emit):
    for place in range(2):

        @pl.when(core == place)
        def _():
            emit(place)


def region(coords, total):
    return jnp.where(coords < total - WIN, 0, jnp.where(coords < total - SHIFT, 1, 2)).astype(
        jnp.int32
    )


def column(row, copies):
    block = jnp.broadcast_to(row, (128, row.shape[1])).T
    return jnp.concatenate([block] * copies, axis=1)


def same_region(place_ref, window, totals):
    tokens = WIN * WIN

    def labels(shape, dim):
        token = lax.broadcasted_iota(jnp.int32, shape, dim)
        down = place_ref[1] + window * WIN + token % (tokens // 2) // SHIFT
        along = place_ref[2] + token // (tokens // 2) * SHIFT + token % SHIFT
        return 3 * region(down, totals[0]) + region(along, totals[1])

    return (labels((tokens, tokens), 0) == labels((tokens, tokens), 1)).astype(F32)


def forward_kernel(
    totals, place_ref, x_own_ref, x_own_next_ref, x_side_ref, x_side_next_ref, x_below_ref, x_corner_ref, qkv_ref, proj_ref, gain1_ref, gain2_ref,
    heads_ref, mixed_ref, act1_ref, normed1_ref, inv1_ref, lse_ref, normed2_ref, inv2_ref, act2_ref,
    mask_ref,
):
    channels = x_own_ref.shape[1]
    head_dim = channels // HEADS
    last = pl.program_id(0) == pl.num_programs(0) - 1
    pieces = [
        x_own_ref[...].astype(F32),
        jnp.where(last, x_below_ref[...].astype(F32), x_own_next_ref[...].astype(F32)),
        x_side_ref[...].astype(F32),
        jnp.where(last, x_corner_ref[...].astype(F32), x_side_next_ref[...].astype(F32)),
    ]
    x = jnp.concatenate(pieces, axis=0).T
    normed1, inverse1 = norm_stats(x)
    act1 = (normed1 * column(gain1_ref[...], 2)).astype(BF16)
    act1_ref[...] = act1
    normed1_ref[...] = normed1
    inv1_ref[...] = inverse1
    queries = nn(qkv_ref[pl.ds(0, channels), :], act1) * (head_dim ** (-0.5))
    heads_ref[pl.ds(0, channels), :] = queries.astype(BF16)
    heads_ref[pl.ds(channels, 2 * channels), :] = nn(
        qkv_ref[pl.ds(channels, 2 * channels), :], act1
    ).astype(BF16)
    mask_ref[...] = same_region(place_ref, pl.program_id(0), totals)

    def score(head):
        at = head * head_dim
        return tn(heads_ref[pl.ds(channels + at, head_dim), :], heads_ref[pl.ds(at, head_dim), :])

    def soften(head, scores):
        scores = jnp.where(mask_ref[...] > 0.5, scores, MASKED)
        highest = jnp.max(scores, axis=0, keepdims=True)
        raised = jnp.exp(scores - highest)
        total = jnp.sum(raised, axis=0, keepdims=True)
        lse_ref[0, pl.ds(head, 1), :] = highest + jnp.log(total)
        return raised.astype(BF16), 1.0 / total

    def mix(head, pair):
        raised, scale = pair
        at = head * head_dim
        value = heads_ref[pl.ds(2 * channels + at, head_dim), :]
        mixed_ref[pl.ds(at, head_dim), :] = (nn(value, raised) * scale).astype(BF16)

    staged(HEADS, 2, score, soften, mix)
    attn = nn(proj_ref[...], mixed_ref[...]).astype(BF16)
    normed2, inverse2 = norm_stats(x + attn.astype(F32))
    normed2_ref[...] = normed2
    inv2_ref[...] = inverse2
    act2_ref[...] = (normed2 * column(gain2_ref[...], 2)).astype(BF16)


def forward(totals, place, x_own, x_side, x_below, x_corner, qkv_weight, proj_weight, gain1, gain2):
    quarter, channels = x_below.shape
    tokens = 2 * (x_own.shape[0] + quarter)
    window = WIN * WIN
    windows = tokens // window
    whole = lambda shape: pl.BlockSpec(shape, lambda w: (0,) * len(shape))
    feature = lambda rows: pl.BlockSpec((rows, window), lambda w: (0, w))
    here = pl.BlockSpec((quarter, channels), lambda w: (2 * w, 0))
    following = pl.BlockSpec(
        (quarter, channels), lambda w: (jnp.minimum(2 * w + 1, 2 * windows - 2), 0)
    )
    return pl.pallas_call(
        functools.partial(forward_kernel, totals),
        grid=(windows,),
        in_specs=[
            pl.BlockSpec(memory_space=pltpu.SMEM),
            here,
            following,
            here,
            following,
            whole(x_below.shape),
            whole(x_corner.shape),
            whole(qkv_weight.shape),
            whole(proj_weight.shape),
            whole((1, channels)),
            whole((1, channels)),
        ],
        out_specs=[
            feature(3 * channels),
            feature(channels),
            feature(channels),
            feature(channels),
            feature(1),
            pl.BlockSpec((1, HEADS, window), lambda w: (w, 0, 0)),
            feature(channels),
            feature(1),
            feature(channels),
        ],
        out_shape=[
            jax.ShapeDtypeStruct((3 * channels, tokens), BF16),
            jax.ShapeDtypeStruct((channels, tokens), BF16),
            jax.ShapeDtypeStruct((channels, tokens), BF16),
            jax.ShapeDtypeStruct((channels, tokens), F32),
            jax.ShapeDtypeStruct((1, tokens), F32),
            jax.ShapeDtypeStruct((windows, HEADS, window), F32),
            jax.ShapeDtypeStruct((channels, tokens), F32),
            jax.ShapeDtypeStruct((1, tokens), F32),
            jax.ShapeDtypeStruct((channels, tokens), BF16),
        ],
        scratch_shapes=[pltpu.VMEM((window, window), F32)],
        compiler_params=pltpu.CompilerParams(vmem_limit_bytes=64 * 2**20),
        name="attention_forward",
    )(
        place, x_own, x_own, x_side, x_side, x_below, x_corner, qkv_weight, proj_weight,
        gain1[None, :], gain2[None, :],
    )


def feed_forward_kernel(
    core_ref, g_own_ref, g_side_ref, g_below_ref, g_corner_ref, act2_ref, gain2_ref, fc1_ref, fc2_ref,
    mine_ref, other_ref, grad_act2_ref, gain_ref, g_t_ref,
    fc2_sum_ref, active_ref, grad_hidden_ref,
):
    step = pl.program_id(0)
    core = core_ref[0]
    channels, tokens = act2_ref.shape
    chunk = fc1_ref.shape[0]
    rows = 32
    piece = 256

    @pl.when(step == 0)
    def _():
        half = WIN * SHIFT
        halves = [(g_own_ref, g_below_ref), (g_side_ref, g_corner_ref)]
        for window in range(tokens // (2 * half)):
            at = window * half
            pieces = []
            for ref, last_ref in halves:
                if at + half <= ref.shape[0]:
                    pieces.append(ref[pl.ds(at, half), :])
                else:
                    pieces += [ref[pl.ds(at, half // 2), :], last_ref[...]]
            joined = jnp.concatenate([piece.astype(F32) for piece in pieces], axis=0)
            g_t_ref[:, pl.ds(2 * at, 2 * half)] = joined.T.astype(BF16)
        grad_act2_ref[...] = jnp.zeros_like(grad_act2_ref)
        gain_ref[...] = jnp.zeros_like(gain_ref)

    def project(index):
        span = pl.ds(index * piece, piece)
        return nn(fc1_ref[...], act2_ref[:, span]), tn(fc2_ref[...], g_t_ref[:, span])

    def bend(index, pair):
        span = pl.ds(index * piece, piece)
        hidden, grad_active = pair
        grad_active = grad_active.astype(BF16).astype(F32)
        bell = 0.5 * (1.0 + lax.erf(hidden * ROOT_HALF))
        slope = bell + hidden * INV_ROOT_TAU * jnp.exp(-0.5 * hidden * hidden)
        grad_hidden = (grad_active * slope).astype(BF16)
        active_ref[:, span] = (hidden * bell).astype(BF16)
        grad_hidden_ref[:, span] = grad_hidden
        return grad_hidden

    def back(index, grad_hidden):
        grad_act2_ref[:, pl.ds(index * piece, piece)] += tn(fc1_ref[...], grad_hidden)

    staged(tokens // piece, 1, project, bend, back)
    fc1_part = nt(grad_hidden_ref[...], act2_ref[...])
    gain_ref[...] += jnp.sum(
        fc1_part * fc1_ref[...].astype(F32), axis=0, keepdims=True
    ) / gain2_ref[...]
    fc1_low = fc1_part.astype(BF16)
    fc2_sum_ref[step] = nt(g_t_ref[...], active_ref[...])

    def emit_fc1(place):
        for group in range(chunk // 16):
            at = step * (chunk // 32 * rows) + (group // 2) * rows
            to = pl.ds(pl.multiple_of(at, rows), 16)
            ref = mine_ref if group % 2 == place else other_ref
            ref[to, :] = fc1_low[group * 16 : (group + 1) * 16]

    by_place(core, emit_fc1)

    def emit_fc2(place):
        @pl.loop(0, channels // 8)
        def _(pair):
            at = pl.ds(pl.multiple_of(pair * 8, 8), 8)
            taken = [fc2_sum_ref[s, at, :] for s in range(4)]
            to = pl.ds(pl.multiple_of(pair * rows + 16, 16), 16)
            for half in range(2):
                block = jnp.concatenate([t[4 * half : 4 * half + 4] for t in taken], axis=0)
                ref = mine_ref if half == place else other_ref
                ref[to, :] = block.astype(BF16)

    @pl.when(step == pl.num_programs(0) - 1)
    def _():
        by_place(core, emit_fc2)


def feed_forward(core, g_own, g_side, g_below, g_corner, act2, gain2, fc1_weight, fc2_weight):
    channels, tokens = act2.shape
    hidden = fc1_weight.shape[0]
    chunk = hidden // 4
    whole = lambda shape: pl.BlockSpec(shape, lambda s: (0,) * len(shape))
    return pl.pallas_call(
        feed_forward_kernel,
        grid=(hidden // chunk,),
        in_specs=[
            pl.BlockSpec(memory_space=pltpu.SMEM),
            whole(g_own.shape),
            whole(g_side.shape),
            whole(g_below.shape),
            whole(g_corner.shape),
            whole((channels, tokens)),
            whole((1, channels)),
            pl.BlockSpec((chunk, channels), lambda s: (s, 0)),
            pl.BlockSpec((channels, chunk), lambda s: (0, s)),
        ],
        out_specs=[
            whole((hidden, channels)),
            whole((hidden, channels)),
            whole((channels, tokens)),
            whole((1, channels)),
            whole((channels, tokens)),
        ],
        out_shape=[
            jax.ShapeDtypeStruct((hidden, channels), BF16),
            jax.ShapeDtypeStruct((hidden, channels), BF16),
            jax.ShapeDtypeStruct((channels, tokens), F32),
            jax.ShapeDtypeStruct((1, channels), F32),
            jax.ShapeDtypeStruct((channels, tokens), BF16),
        ],
        scratch_shapes=[
            pltpu.VMEM((hidden // chunk, channels, chunk), F32),
            pltpu.VMEM((chunk, tokens), BF16),
            pltpu.VMEM((chunk, tokens), BF16),
        ],
        compiler_params=pltpu.CompilerParams(vmem_limit_bytes=64 * 2**20),
        name="feed_forward",
    )(core, g_own, g_side, g_below, g_corner, act2, gain2[None, :], fc1_weight, fc2_weight)


def backward_kernel(
    totals, place_ref, g_t_ref, grad_act2_ref, normed2_ref, inv2_ref, heads_ref, mixed_ref, lse_ref, act1_ref,
    normed1_ref, inv1_ref, gain1_ref, gain2_ref, gain2_sum_ref, qkv_ref, proj_ref,
    dx_left_ref, dx_right_ref, mine_ref, other_ref,
    mask_ref, grad_mixed_ref, grad_heads_ref, qkv_sum_ref, proj_sum_ref, qkv_t_ref, proj_t_ref, gains_ref,
):
    step = pl.program_id(0)
    channels = grad_act2_ref.shape[0]
    head_dim = channels // HEADS

    @pl.when(step == 0)
    def _():
        qkv_sum_ref[...] = jnp.zeros_like(qkv_sum_ref)
        proj_sum_ref[...] = jnp.zeros_like(proj_sum_ref)
        qkv_t_ref[...] = qkv_ref[...].T
        proj_t_ref[...] = proj_ref[...].T

    mask_ref[...] = same_region(place_ref, step, totals)
    resid = g_t_ref[...].astype(F32) + norm_back(
        grad_act2_ref[...] * column(gain2_ref[...], 2), normed2_ref[...], inv2_ref[...]
    )
    low = resid.astype(BF16)
    grad_mixed_ref[...] = nn(proj_t_ref[...], low).astype(BF16)
    proj_sum_ref[...] += nt(low, mixed_ref[...])

    def spans(head):
        at = head * head_dim
        return [pl.ds(group * channels + at, head_dim) for group in range(3)]

    def score(head):
        q, k, v = spans(head)
        return (
            tn(heads_ref[k, :], heads_ref[q, :]),
            tn(heads_ref[v, :], grad_mixed_ref[q, :]),
        )

    def soften(head, pair):
        scores, grad_probs = pair
        scores = jnp.where(mask_ref[...] > 0.5, scores, MASKED)
        probs = jnp.exp(scores - lse_ref[0, pl.ds(head, 1), :])
        own = spans(head)[0]
        cross = jnp.sum(
            grad_mixed_ref[own, :].astype(F32) * mixed_ref[own, :].astype(F32), axis=0, keepdims=True
        )
        return probs.astype(BF16), (probs * (grad_probs - cross)).astype(BF16)

    def mix(head, pair):
        probs_low, scores_low = pair
        q, k, v = spans(head)
        grad_heads_ref[v, :] = nt(grad_mixed_ref[q, :], probs_low).astype(BF16)
        grad_heads_ref[q, :] = (nn(heads_ref[k, :], scores_low) * (head_dim ** (-0.5))).astype(BF16)
        grad_heads_ref[k, :] = nt(heads_ref[q, :], scores_low).astype(BF16)

    staged(HEADS, 1, score, soften, mix)
    grad_act1 = nn(qkv_t_ref[...], grad_heads_ref[...]).astype(BF16).astype(F32)
    qkv_sum_ref[...] += nt(grad_heads_ref[...], act1_ref[...])
    dx = resid + norm_back(grad_act1 * column(gain1_ref[...], 2), normed1_ref[...], inv1_ref[...])
    dx = dx.T.astype(BF16)
    half = dx.shape[0] // 2
    dx_left_ref[...] = dx[:half]
    dx_right_ref[...] = dx[half:]

    def emit(place):
        @pl.loop(0, channels // 16)
        def _(four):
            at = pl.ds(pl.multiple_of(four * 16, 16), 16)
            qkv = qkv_sum_ref[pl.ds(pl.multiple_of(four * 48, 16), 48), :]
            proj = proj_sum_ref[at, :]
            gain = gains_ref[at, :]
            zeros = jnp.zeros((4, 128), F32)
            for half in range(2):
                ref = mine_ref if half == place else other_ref
                tops, lows, sides = [], [], []
                for pair in range(2):
                    device = 2 * pair + half
                    rows = qkv[12 * device : 12 * device + 12]
                    tops.append(rows[:8])
                    lows += [rows[8:], proj[4 * device : 4 * device + 4]]
                    sides += [zeros, gain[4 * device : 4 * device + 4]]
                for index, blocks in enumerate((tops, lows, sides)):
                    block = jnp.concatenate(blocks, axis=0).astype(BF16)
                    ref[at, pl.ds(index * channels, block.shape[1])] = block

    @pl.when(step == pl.num_programs(0) - 1)
    def _():
        gain1_sum = jnp.sum(
            qkv_sum_ref[...] * qkv_ref[...].astype(F32), axis=0, keepdims=True
        ) / gain1_ref[...]
        lines = lax.broadcasted_iota(jnp.int32, (128, channels), 0)
        gains_ref[...] = jnp.where(
            lines == 0, gain1_sum, jnp.where(lines == 1, gain2_sum_ref[...], 0.0)
        ).T
        by_place(place_ref[0], emit)


def backward(
    totals, place, g_t, grad_act2, normed2, inv2, heads, mixed, lse, act1, normed1, inv1,
    gain1, gain2, gain2_sum, qkv_weight, proj_weight,
):
    channels, tokens = grad_act2.shape
    window = WIN * WIN
    windows = tokens // window
    whole = lambda shape: pl.BlockSpec(shape, lambda w: (0,) * len(shape))
    feature = lambda rows: pl.BlockSpec((rows, window), lambda w: (0, w))
    packed = (channels, 2 * channels + 128)
    return pl.pallas_call(
        functools.partial(backward_kernel, totals),
        grid=(windows,),
        in_specs=[
            pl.BlockSpec(memory_space=pltpu.SMEM),
            feature(channels),
            feature(channels),
            feature(channels),
            feature(1),
            feature(3 * channels),
            feature(channels),
            pl.BlockSpec((1, HEADS, window), lambda w: (w, 0, 0)),
            feature(channels),
            feature(channels),
            feature(1),
            whole((1, channels)),
            whole((1, channels)),
            whole((1, channels)),
            whole(qkv_weight.shape),
            whole(proj_weight.shape),
        ],
        out_specs=[
            pl.BlockSpec((window // 2, channels), lambda w: (w, 0)),
            pl.BlockSpec((window // 2, channels), lambda w: (w, 0)),
            whole(packed),
            whole(packed),
        ],
        out_shape=[
            jax.ShapeDtypeStruct((tokens // 2, channels), BF16),
            jax.ShapeDtypeStruct((tokens // 2, channels), BF16),
            jax.ShapeDtypeStruct(packed, BF16),
            jax.ShapeDtypeStruct(packed, BF16),
        ],
        scratch_shapes=[
            pltpu.VMEM((window, window), F32),
            pltpu.VMEM((channels, window), BF16),
            pltpu.VMEM((3 * channels, window), BF16),
            pltpu.VMEM((3 * channels, channels), F32),
            pltpu.VMEM((channels, channels), F32),
            pltpu.VMEM((channels, 3 * channels), BF16),
            pltpu.VMEM((channels, channels), BF16),
            pltpu.VMEM((channels, 128), F32),
        ],
        compiler_params=pltpu.CompilerParams(vmem_limit_bytes=64 * 2**20),
        cost_estimate=pl.CostEstimate(
            flops=30 * tokens * channels * window,
            bytes_accessed=20 * tokens * channels,
            transcendentals=HEADS * tokens * window,
        ),
        name="attention_backward",
    )(
        place, g_t, grad_act2, normed2, inv2, heads, mixed, lse, act1, normed1, inv1,
        gain1[None, :], gain2[None, :], gain2_sum, qkv_weight, proj_weight,
    )


def unpack_kernel(factor, pieces_ref, qkv_out_ref, proj_out_ref, gain1_out_ref, gain2_out_ref, sum_ref):
    step = pl.program_id(0)

    @pl.when(step == 0)
    def _():
        sum_ref[...] = jnp.zeros_like(sum_ref)

    total = sum_ref[...]
    for piece in range(pieces_ref.shape[0]):
        total += pieces_ref[piece].astype(F32)
    sum_ref[...] = total

    @pl.when(step == pl.num_programs(0) - 1)
    def _():
        rows, channels = qkv_out_ref.shape
        scaled = sum_ref[...] * factor
        height = scaled.shape[0]
        rest = rows - height
        qkv_out_ref[pl.ds(0, height), :] = scaled[:, :channels]
        qkv_out_ref[pl.ds(height, rest), :] = scaled[:rest, channels : 2 * channels]
        proj_out_ref[...] = scaled[rest:, channels : 2 * channels]
        gains = jnp.concatenate([scaled[:, 2 * channels :]] * 16, axis=0).T
        gain1_out_ref[...] = gains[0:1, rest:height]
        gain2_out_ref[...] = gains[1:2, rest:height]


def unpack(pieces, rows, factor):
    chips, both, columns = pieces.shape
    channels = (columns - 128) // 2
    rest = 2 * both - rows
    shapes = [(rows, channels), (rest, channels), (1, rest), (1, rest)]
    return pl.pallas_call(
        functools.partial(unpack_kernel, factor),
        grid=(2,),
        in_specs=[pl.BlockSpec((chips // 2, both, columns), lambda s: (s, 0, 0))],
        out_specs=[pl.BlockSpec(shape, lambda s: (0, 0)) for shape in shapes],
        out_shape=[jax.ShapeDtypeStruct(shape, F32) for shape in shapes],
        scratch_shapes=[pltpu.VMEM((both, columns), F32)],
        compiler_params=pltpu.CompilerParams(vmem_limit_bytes=64 * 2**20),
        name="unpack",
    )(pieces)


def unpack_ffn_kernel(factor, pieces_ref, fc1_out_ref, fc2_out_ref, sum_ref):
    step = pl.program_id(0)

    @pl.when(step == 0)
    def _():
        sum_ref[...] = jnp.zeros_like(sum_ref)

    total = sum_ref[...]
    for piece in range(pieces_ref.shape[0]):
        total += pieces_ref[piece].astype(F32)
    sum_ref[...] = total

    @pl.when(step == pl.num_programs(0) - 1)
    def _():
        rows, channels = fc1_out_ref.shape
        scaled = sum_ref[...] * factor
        fc1_out_ref[...] = scaled[:rows]
        for part in range(fc2_out_ref.shape[1] // channels):
            at = rows + 4 * part
            fc2_out_ref[:, pl.ds(part * channels, channels)] = scaled[at : at + 4]


def unpack_ffn(pieces, fc1_rows, factor):
    chips, rows, channels = pieces.shape
    fc2_rows = (rows - fc1_rows) // 4
    shapes = [(fc1_rows, channels), (fc2_rows, 4 * channels)]
    return pl.pallas_call(
        functools.partial(unpack_ffn_kernel, factor),
        grid=(4,),
        in_specs=[pl.BlockSpec((chips // 4, rows, channels), lambda s: (s, 0, 0))],
        out_specs=[pl.BlockSpec(shape, lambda s: (0, 0)) for shape in shapes],
        out_shape=[jax.ShapeDtypeStruct(shape, F32) for shape in shapes],
        scratch_shapes=[pltpu.VMEM((rows, channels), F32)],
        compiler_params=pltpu.CompilerParams(vmem_limit_bytes=64 * 2**20),
        cost_estimate=pl.CostEstimate(
            flops=2**30, bytes_accessed=2 * chips * rows * channels, transcendentals=0
        ),
        name="unpack_ffn",
    )(pieces)


def diagonal(block, distance):
    rows = lax.axis_size("zl") * lax.axis_size("y")
    cols = lax.axis_size("zh") * lax.axis_size("x") * lax.axis_size("core")
    route = [
        ((r - distance) % rows * cols + (c - distance) % cols, r * cols + c) for r in range(rows) for c in range(cols)
    ]
    return lax.ppermute(block, ALL, route)


def roll_out(left, right):
    before = ring(right, COLS, 1)[:-SHIFT]
    above = ring(left[-SHIFT:], ROWS, 1)
    corner = diagonal(right[-SHIFT:], 1)
    top = jnp.concatenate([corner, above], axis=1)
    rest = jnp.concatenate([before, left[:-SHIFT]], axis=1)
    return jnp.concatenate([top, rest], axis=0)


def core_sum(mine, other):
    got = lax.ppermute(other, "core", [(0, 1), (1, 0)])
    return (mine.astype(F32) + got.astype(F32)).astype(BF16)


def chips_exchange(part):
    chips = 1
    for axis in CHIPS:
        chips *= lax.axis_size(axis)
    return lax.all_to_all(part.reshape(chips, -1, part.shape[1]), CHIPS, 0, 0, tiled=True)


def shards(tokens, cotangent, gain1, qkv_weight, proj_weight, gain2, fc1_weight, fc2_weight):
    tile_rows, tile_cols, channels = tokens.shape
    devices = 1
    for axis in ALL:
        devices *= lax.axis_size(axis)
    rows_total = tile_rows * lax.axis_size("zl") * lax.axis_size("y")
    cols_total = tile_cols * (devices * tile_rows // rows_total)
    totals = (rows_total, cols_total)
    place = jnp.stack(
        [
            lax.axis_index("core"),
            lax.axis_index(ROWS) * tile_rows,
            lax.axis_index(COLS) * tile_cols,
        ]
    ).astype(jnp.int32)
    flat = lambda block: block.reshape(-1, channels)
    x_out, tokens, cotangent = lax.optimization_barrier((tokens[SHIFT:, :SHIFT], tokens, cotangent))
    x_side = flat(ring(x_out, COLS, -1))
    first = jnp.stack([tokens[:SHIFT], cotangent[:SHIFT]])
    below = ring(first[:, :, SHIFT:], ROWS, -1)
    corner = diagonal(first[:, :, :SHIFT], -1)
    g_side = flat(ring(cotangent[SHIFT:, :SHIFT], COLS, -1))
    x_own = flat(tokens[SHIFT:, SHIFT:])
    g_own = flat(cotangent[SHIFT:, SHIFT:])
    heads, mixed, act1, normed1, inv1, lse, normed2, inv2, act2 = forward(
        totals, place, x_own, x_side, flat(below[0]), flat(corner[0]), qkv_weight, proj_weight,
        gain1, gain2,
    )
    ffn_mine, ffn_other, grad_act2, gain2_sum, g_t = feed_forward(
        place, g_own, g_side, flat(below[1]), flat(corner[1]), act2, gain2, fc1_weight, fc2_weight
    )
    ffn_chip = core_sum(ffn_mine, ffn_other)
    grad_act2, ffn_chip = lax.optimization_barrier((grad_act2, ffn_chip))
    ffn_pieces = chips_exchange(ffn_chip)
    dx_left, dx_right, att_mine, att_other = backward(
        totals, place, g_t, grad_act2, normed2, inv2, heads, mixed, lse, act1, normed1, inv1,
        gain1, gain2, gain2_sum, qkv_weight, proj_weight,
    )
    halves = (tile_rows, SHIFT, channels)
    grad_tokens = roll_out(dx_left.reshape(halves), dx_right.reshape(halves))
    att_chip = core_sum(att_mine, att_other)
    att_chip, grad_tokens = lax.optimization_barrier((att_chip, grad_tokens))
    norm_factor = (rows_total * cols_total) ** (-0.5)
    qkv_rows = qkv_weight.shape[0] // devices
    qkv_out, proj_out, gain1_out, gain2_out = unpack(
        chips_exchange(att_chip), qkv_rows, norm_factor
    )
    fc1_out, fc2_out = unpack_ffn(ffn_pieces, fc1_weight.shape[0] // devices, norm_factor)
    return (
        grad_tokens,
        qkv_out,
        proj_out,
        fc1_out,
        fc2_out,
        gain1_out.reshape(-1),
        gain2_out.reshape(-1),
    )


def solution(mesh):
    fine = Mesh(mesh.devices.reshape(2, 4, 2, 4, 2), ALL)
    return jax.shard_map(
        shards,
        mesh=fine,
        in_specs=(P(ROWS, COLS, None), P(ROWS, COLS, None), P(), P(), P(), P(), P(), P()),
        out_specs=(
            P(ROWS, COLS, None),
            P(ALL, None),
            P(ALL, None),
            P(ALL, None),
            P(ALL, None),
            P(ALL),
            P(ALL),
        ),
        check_vma=False,
    )
```
